32 devices in a mesh: section: 4 (over y, x), expert: 8 (over z, core).
Axes of the slice: x: 2, y: 2, z: 4, core: 2. Of those that a mesh axis runs over, the one named last changes fastest.
Arguments:
- grad_out: bfloat16 [4, 512, 2048], P('section', 'expert'), may hold values from -3 to 3
- pre_act: bfloat16 [4, 512, 2, 2, 768], P('section', 'expert'), may hold values from -5 to 5
- route_ids: int32 [4, 512, 2], P('section', 'expert'), may hold values from 0 to 7, as said below
- route_gate: bfloat16 [4, 512, 2], P('section', 'expert'), may hold values from 0.19921875 to 1
- w_gate: bfloat16 [4, 2048, 6144], P('section', None, 'expert'), may hold values from -0.125 to 0.125
- w_up: bfloat16 [4, 2048, 6144], P('section', None, 'expert'), may hold values from -0.125 to 0.125
- w_down: bfloat16 [4, 6144, 2048], P('section', 'expert'), may hold values from -0.21875 to 0.21875
Outputs:
- grad_in: bfloat16 [4, 512, 2048], P('section', 'expert')
- grad_down: bfloat16 [4, 6144, 2048], P('section', 'expert')
The draws below stay inside these ranges and needn't reach their ends.
Inputs may be any that keep to these rules, and one draw needn't show every extreme that they name: `route_ids`: each row names 2 different experts. In the rows of one device of one section (aligned blocks of 64 tokens) no expert is named by more than 24 rows, and in every block one expert is named by exactly 24 rows.
All inputs are finite; a program needn't handle non-finite values.
Results may differ from the reference program's by a relative error of at most 0.0065.
Values may be sent and summed in bfloat16 or wider, within the bound.
No kernel may reach another device: no remote copies, remote signals or barrier semaphores. Data moves between devices by JAX's collectives and lax.ppermute only.
A program may use at most 64 MiB of HBM per device.

```python
import jax
import jax.numpy as jnp
from jax import lax

D = 2048
FF = 768
EXPERTS = 8
TOPK = 2
TOK_DEV = 64
SECTIONS = 4
TOKENS = 512
CAP = 24
N_EXPERT = 8


def route_block(key, hot_expert):
    key_hot, key_cold, key_flip, key_perm = jax.random.split(key, 4)
    others = EXPERTS - 1
    offset_hot = jax.random.randint(key_hot, (), 0, others)
    offset_cold = jax.random.randint(key_cold, (), 0, others)
    slot_rank = jnp.arange(TOK_DEV)
    in_hot = slot_rank < CAP
    cold_index = slot_rank - CAP
    hot_second = (hot_expert + 1 + (slot_rank + offset_hot) % others) % EXPERTS
    cold_first = (hot_expert + 1 + (2 * cold_index + offset_cold) % others) % EXPERTS
    cold_second = (hot_expert + 1 + (2 * cold_index + 1 + offset_cold) % others) % EXPERTS
    first_pick = jnp.where(in_hot, hot_expert, cold_first)
    second_pick = jnp.where(in_hot, hot_second, cold_second)
    flipped = jax.random.randint(key_flip, (TOK_DEV,), 0, 2)
    forward_pair = jnp.stack([first_pick, second_pick], axis=1)
    reverse_pair = jnp.stack([second_pick, first_pick], axis=1)
    pairs = jnp.where(flipped[:, None] == 1, reverse_pair, forward_pair)
    row_order = jax.random.permutation(key_perm, TOK_DEV)
    return pairs[row_order]


def draw_route_ids(key, part):
    per_section = TOKENS // TOK_DEV
    block_total = SECTIONS * per_section
    key_hot, key_blocks = jax.random.split(jax.random.fold_in(key, 17))
    hot_blocks = jax.random.randint(key_hot, (block_total,), 0, EXPERTS)
    block_keys = jax.random.split(key_blocks, block_total)
    rows_all = jax.vmap(route_block)(block_keys, hot_blocks)
    return rows_all.reshape(SECTIONS, TOKENS, TOPK).astype(jnp.int32)


def block_scale(own_key, extent, cuts, low, largest):
    factor_of = 1.0
    for dim, shards_of in cuts:
        steps = jax.random.uniform(jax.random.fold_in(jax.random.fold_in(own_key, 6), dim), (shards_of,), jnp.float32, low / len(cuts), largest / len(cuts))
        factor_of = factor_of * jnp.repeat(jnp.exp(steps), extent[dim] // shards_of).reshape((-1,) + (1,) * (len(extent) - 1 - dim))
    return factor_of


def scatter_about(own_key, shape, width, bound, cuts=(), held_as=jnp.bfloat16):
    values = jax.random.normal(own_key, shape, jnp.float32) * width
    if len(cuts) > 0:
        values = block_scale(own_key, shape, cuts, -0.22, 0.18) * values
    return jnp.clip(values, min=-bound, max=bound).astype(held_as)


def setup_inputs(seed: int = 0) -> dict:
    key_list = jax.random.split(jax.random.key(seed), 8)
    grad_out = scatter_about(key_list[0], (SECTIONS, TOKENS, D), 0.5, 3.0, ((0, 4), (1, 8)))
    pre_act = scatter_about(key_list[1], (SECTIONS, TOKENS, TOPK, 2, FF), 1.0, 5.0, ((0, 4), (1, 8)))
    route_ids = draw_route_ids(jax.random.fold_in(key_list[7], 71), 0)
    route_gate = jnp.clip(0.19921875 + 0.80078125 * jax.random.uniform(key_list[3], (SECTIONS, TOKENS, TOPK), jnp.float32) ** block_scale(key_list[3], (SECTIONS, TOKENS, TOPK), ((0, 4), (1, 8)), -0.2, 0.2), 0.19921875, 1.0).astype(jnp.bfloat16)
    w_gate = scatter_about(key_list[4], (SECTIONS, D, EXPERTS * FF), D ** -0.5, 0.125, ((0, 4), (2, 8)))
    w_up = scatter_about(key_list[5], (SECTIONS, D, EXPERTS * FF), D ** -0.5, 0.125, ((0, 4), (2, 8)))
    w_down = scatter_about(key_list[6], (SECTIONS, EXPERTS * FF, D), FF ** -0.5, 0.21875, ((0, 4), (1, 8)))
    return dict(grad_out=grad_out, pre_act=pre_act, route_ids=route_ids, route_gate=route_gate, w_gate=w_gate, w_up=w_up, w_down=w_down)


def section_grads(inputs):
    upstream, saved_acts, route_rows, gate_vals, weight_gate, weight_up, weight_down = inputs
    block_total = TOKENS // TOK_DEV
    group_size = N_EXPERT // EXPERTS
    hid_units = FF // group_size
    picked = route_rows[:, :, None] == jnp.arange(EXPERTS, dtype=jnp.int32)[None, None, :]
    is_named = jnp.any(picked, axis=1).reshape(block_total, TOK_DEV, EXPERTS).astype(jnp.int32)
    slot_rank = jnp.cumsum(is_named, axis=1) - 1
    slot_index = jnp.where(is_named > 0, slot_rank, -1)
    upstream_f = upstream.reshape(block_total, TOK_DEV, D).astype(jnp.float32)
    token_grad = jnp.zeros((block_total, TOK_DEV, D), jnp.float32)
    down_parts = []
    high = lax.Precision.HIGHEST
    for expert_no in range(EXPERTS):
        selector = (slot_index[:, :, expert_no][:, None, :] == jnp.arange(CAP, dtype=jnp.int32)[None, :, None]).astype(jnp.float32)
        rows_up = jnp.einsum("bct,btd->bcd", selector, upstream_f, precision=high).reshape(-1, D).astype(jnp.bfloat16)
        gate_sel = jnp.sum(jnp.where(picked[:, :, expert_no], gate_vals.astype(jnp.float32), 0.0), axis=1)
        rows_gate = jnp.einsum("bct,bt->bc", selector, gate_sel.reshape(block_total, TOK_DEV), precision=high).reshape(-1)
        saved_sel = jnp.zeros((TOKENS, 2, FF), jnp.float32)
        for pick_index in range(TOPK):
            saved_sel = jnp.where(picked[:, pick_index, expert_no][:, None, None], saved_acts[:, pick_index].astype(jnp.float32), saved_sel)
        rows_saved = jnp.einsum("bct,btx->bcx", selector, saved_sel.reshape(block_total, TOK_DEV, 2 * FF), precision=high).reshape(-1, 2 * FF)
        gate_pre = rows_saved[:, :FF]
        up_pre = rows_saved[:, FF:]
        low_col = expert_no * FF
        down_block = weight_down[low_col:low_col + FF]
        gate_block = weight_gate[:, low_col:low_col + FF]
        up_block = weight_up[:, low_col:low_col + FF]
        grad_hidden = jnp.dot(rows_up, down_block.T, preferred_element_type=jnp.float32) * rows_gate[:, None]
        sigmoid_g = jax.nn.sigmoid(gate_pre)
        silu_val = gate_pre * sigmoid_g
        grad_gate = (grad_hidden * up_pre * sigmoid_g * (1.0 + gate_pre * (1.0 - sigmoid_g))).astype(jnp.bfloat16)
        grad_upper = (grad_hidden * silu_val).astype(jnp.bfloat16)
        scaled_hidden = (rows_gate[:, None] * silu_val * up_pre).astype(jnp.bfloat16)
        down_parts.append(jnp.dot(scaled_hidden.T, rows_up, preferred_element_type=jnp.float32).astype(jnp.bfloat16))
        summed = jnp.zeros((block_total * CAP, D), jnp.float32)
        for member_no in range(group_size):
            low_unit = member_no * hid_units
            slice_term = jnp.dot(grad_gate[:, low_unit:low_unit + hid_units], gate_block[:, low_unit:low_unit + hid_units].T, preferred_element_type=jnp.float32)
            slice_term = slice_term + jnp.dot(grad_upper[:, low_unit:low_unit + hid_units], up_block[:, low_unit:low_unit + hid_units].T, preferred_element_type=jnp.float32)
            rounded = lax.optimization_barrier(slice_term.astype(jnp.bfloat16))
            summed = summed + rounded.astype(jnp.float32)
        member_total = lax.optimization_barrier(summed.astype(jnp.bfloat16)).astype(jnp.float32)
        token_grad = token_grad + jnp.einsum("bct,bcd->btd", selector, member_total.reshape(block_total, CAP, D), precision=high)
    return token_grad.reshape(TOKENS, D).astype(jnp.bfloat16), jnp.concatenate(down_parts, axis=0)


def reference(grad_out, pre_act, route_ids, route_gate, w_gate, w_up, w_down):
    token_grads, grad_down = lax.map(section_grads, (grad_out, pre_act, route_ids, route_gate, w_gate, w_up, w_down))
    grad_in = jnp.roll(token_grads, -1, axis=0)
    return grad_in, grad_down
```

```python
import jax
import jax.numpy as jnp
from jax import lax
from jax.sharding import PartitionSpec as P

EXPERTS = 8


def shifted_2(value, axis, steps):
    count = lax.axis_size(axis)
    pairs = [(source, (source + steps) % count) for source in range(count)]
    return lax.ppermute(value, axis, pairs)


def expert_rows(upstream, saved_rows, gate_rows, weight_gate, weight_up, weight_down):
    hid_units = weight_down.shape[0]
    grad_hidden = (
        lax.dot_general(
            upstream, weight_down, (((1,), (1,)), ((), ())), preferred_element_type=jnp.float32
        )
        * gate_rows[:, None]
    )
    saved_f = saved_rows.astype(jnp.float32)
    gate_pre = saved_f[:, :hid_units]
    up_pre = saved_f[:, hid_units:]
    sigmoid_g = jax.nn.sigmoid(gate_pre)
    silu_val = gate_pre * sigmoid_g
    grad_gate = (grad_hidden * up_pre * sigmoid_g * (1.0 + gate_pre * (1.0 - sigmoid_g))).astype(
        jnp.bfloat16
    )
    grad_upper = (grad_hidden * silu_val).astype(jnp.bfloat16)
    scaled_hidden = (gate_rows[:, None] * silu_val * up_pre).astype(jnp.bfloat16)
    contract_last = (((1,), (1,)), ((), ()))
    back_rows = lax.dot_general(
        grad_gate, weight_gate, contract_last, preferred_element_type=jnp.float32
    )
    back_rows = (
        back_rows
        + lax.dot_general(grad_upper, weight_up, contract_last, preferred_element_type=jnp.float32)
    ).astype(jnp.bfloat16)
    weight_term = lax.dot_general(
        scaled_hidden, upstream, (((0,), (0,)), ((), ())), preferred_element_type=jnp.float32
    )
    return (back_rows, weight_term)


def on_device_general(grad_out, pre_act, route_ids, route_gate, w_gate, w_up, w_down):
    member_count = lax.axis_size("expert")
    group_size = member_count // EXPERTS
    token_count = grad_out.shape[1]
    model_width = grad_out.shape[2]
    hid_units = w_down.shape[1]
    slot_cap = 3 * token_count // 8
    part_rows = slot_cap // group_size
    upstream = grad_out[0]
    route_rows = route_ids[0]
    gate_vals = route_gate[0]
    saved_acts = pre_act[0]
    weight_gate = w_gate[0]
    weight_up = w_up[0]
    weight_down = w_down[0]
    picked = route_rows[:, :, None] == jnp.arange(EXPERTS, dtype=jnp.int32)[None, None, :]
    is_named = jnp.any(picked, axis=1).astype(jnp.int32)
    slot_rank = jnp.cumsum(is_named, axis=0) - 1
    slot_index = jnp.where(is_named > 0, slot_rank, -1)
    selector = slot_index.T[:, None, :] == jnp.arange(slot_cap, dtype=jnp.int32)[None, :, None]
    order_sel = selector.reshape(EXPERTS, group_size, part_rows, token_count).transpose(1, 0, 2, 3)
    order_bf = order_sel.astype(jnp.bfloat16)
    gate_sel = jnp.sum(jnp.where(picked, gate_vals[:, :, None].astype(jnp.float32), 0.0), axis=1)
    saved_sel = jnp.zeros((token_count, EXPERTS, 2, saved_acts.shape[3]), jnp.bfloat16)
    for pick_index in range(saved_acts.shape[1]):
        saved_sel = jnp.where(
            picked[:, pick_index, :, None, None], saved_acts[:, pick_index, None, :, :], saved_sel
        )
    saved_rows = jnp.einsum(
        "gect,tex->gecx",
        order_bf,
        saved_sel.reshape(token_count, EXPERTS, -1),
        preferred_element_type=jnp.float32,
    ).astype(jnp.bfloat16)
    saved_rows = saved_rows.reshape(
        group_size, EXPERTS, part_rows, 2, group_size, hid_units
    ).transpose(0, 1, 4, 2, 3, 5)
    saved_buf = saved_rows.reshape(group_size, member_count, part_rows, 2 * hid_units)
    gate_rows = jnp.einsum("gect,te->gec", order_sel.astype(jnp.float32), gate_sel).astype(
        jnp.bfloat16
    )
    gate_buf = jnp.broadcast_to(
        gate_rows[:, :, None, :], (group_size, EXPERTS, group_size, part_rows)
    ).reshape(group_size, member_count, part_rows)
    upstream_rows = jnp.dot(
        order_bf.reshape(-1, token_count), upstream, preferred_element_type=jnp.float32
    ).astype(jnp.bfloat16)
    upstream_rows = upstream_rows.reshape(group_size, EXPERTS, 1, part_rows, model_width)
    upstream_buf = jnp.broadcast_to(
        upstream_rows, (group_size, EXPERTS, group_size, part_rows, model_width)
    )
    upstream_buf = upstream_buf.reshape(group_size, member_count, part_rows, model_width)
    recv_up, recv_saved, recv_gate = (
        lax.all_to_all(upstream_buf, "expert", split_axis=1, concat_axis=1, tiled=True),
        lax.all_to_all(saved_buf, "expert", split_axis=1, concat_axis=1, tiled=True),
        lax.all_to_all(gate_buf, "expert", split_axis=1, concat_axis=1, tiled=True),
    )
    up_flat = recv_up.reshape(-1, model_width)
    saved_flat = recv_saved.reshape(-1, 2 * hid_units)
    gate_flat = recv_gate.reshape(-1)
    gate_f = gate_flat.astype(jnp.float32)
    back_rows, down_sum = expert_rows(
        up_flat, saved_flat, gate_f, weight_gate, weight_up, weight_down
    )
    back_buf = back_rows.reshape(group_size, member_count, part_rows, model_width)
    returned = lax.all_to_all(back_buf, "expert", split_axis=1, concat_axis=1, tiled=True)
    member_sum = (
        returned.astype(jnp.float32)
        .reshape(group_size, EXPERTS, group_size, part_rows, model_width)
        .sum(axis=2)
    )
    summed = lax.optimization_barrier(member_sum.astype(jnp.bfloat16)).astype(jnp.float32)
    token_grad = lax.dot_general(
        order_sel.astype(jnp.float32).reshape(-1, token_count),
        summed.reshape(-1, model_width),
        (((0,), (0,)), ((), ())),
        precision=lax.Precision.HIGHEST,
        preferred_element_type=jnp.float32,
    )
    shifted = shifted_2(token_grad.astype(jnp.bfloat16)[None], "section", -1)
    return (shifted, down_sum.astype(jnp.bfloat16)[None])

def swapped(value, mask):
    count = lax.axis_size("expert")
    return lax.ppermute(value, "expert", [(i, i ^ mask) for i in range(count)])


def slot_ranks(named, tokens):
    lower = jnp.arange(tokens, dtype=jnp.int32)
    upto = (lower[:, None] <= lower[None, :]).astype(jnp.bfloat16)
    counts = jnp.dot(named.astype(jnp.bfloat16), upto, preferred_element_type=jnp.float32)
    return jnp.where(named, counts.astype(jnp.int32) - 1, -1)


def hidden_grads(grad_hidden, saved, gate):
    units = grad_hidden.shape[1]
    saved_f = saved.astype(jnp.float32)
    gate_pre = saved_f[:, :units]
    up_pre = saved_f[:, units:]
    sig = jax.nn.sigmoid(gate_pre)
    silu = gate_pre * sig
    grad_h = grad_hidden * gate
    grad_a = (grad_h * up_pre * sig * (1.0 + gate_pre * (1.0 - sig))).astype(jnp.bfloat16)
    grad_b = (grad_h * silu).astype(jnp.bfloat16)
    scaled = (gate * silu * up_pre).astype(jnp.bfloat16)
    return grad_a, grad_b, scaled


LAST = (((1,), (1,)), ((), ()))
FIRST = (((0,), (0,)), ((), ()))


def on_device_pairs(grad_out, pre_act, route_ids, route_gate, w_gate, w_up, w_down):
    f32, bf16 = jnp.float32, jnp.bfloat16
    tokens, width = grad_out.shape[1:]
    picks = pre_act.shape[2]
    units = w_down.shape[1]
    cap = 3 * tokens // 8
    me = lax.axis_index("expert")
    upstream = grad_out[0]
    meta = jnp.concatenate([route_ids[0].astype(bf16).T, route_gate[0].T], axis=0)
    saved_all = pre_act[0].reshape(tokens * picks, 2 * units)

    far_up = swapped(upstream, 4)
    pair_up = swapped(upstream, 1)
    meta_near = jnp.stack([meta, swapped(meta, 1)])
    meta_far = swapped(meta_near, 4)
    pair_saved = swapped(saved_all, 1)
    far_pair_up = swapped(far_up, 1)

    mine = me ^ jnp.array([0, 2, 4, 6], jnp.int32)

    def selectors(block_meta, experts):
        ids = block_meta[:, :picks].astype(jnp.int32)
        hits = ids[:, None] == experts[None, :, None, None]
        named = jnp.any(hits, axis=2)
        blocks, count = named.shape[:2]
        slots = slot_ranks(named.reshape(-1, tokens), tokens).reshape(named.shape)
        slot_no = jnp.arange(cap, dtype=jnp.int32)[None, None, :, None]
        order = slots[:, :, None, :] == slot_no
        return order, hits

    order_near, hits_near = selectors(meta_near, mine)
    order_far, hits_far = selectors(meta_far, mine[:2])

    def saved_of(block, rows):
        both = order_near[block][:, :, :, None] & jnp.moveaxis(hits_near[block], 1, 2)[:, None]
        sel = both.astype(bf16).reshape(4 * cap, tokens * picks)
        got = jnp.dot(sel, rows, preferred_element_type=f32).astype(bf16)
        return got.reshape(4, cap, 2 * units)

    def gate_of(order, hits, block_meta):
        gates = block_meta[:, None, picks:].astype(f32)
        gate_sel = jnp.sum(jnp.where(hits, gates, 0.0), axis=2)
        got = jnp.sum(jnp.where(order, gate_sel[:, :, None, :], 0.0), axis=3)
        return got

    gates_near = gate_of(order_near, hits_near, meta_near).astype(bf16)
    saved_rows = jnp.stack([saved_of(0, saved_all), saved_of(1, pair_saved)], axis=1)
    gate_cols = jnp.broadcast_to(jnp.moveaxis(gates_near, 0, 1)[..., None], (4, 2, cap, 128))
    packed = jnp.concatenate([saved_rows, gate_cols], axis=3).reshape(4, 2 * cap, 2 * units + 128)

    def up_rows(order, expert, first, second):
        sel = order[:, expert].astype(bf16)
        rows = [
            jnp.dot(sel[n], rows, preferred_element_type=f32).astype(bf16)
            for n, rows in enumerate((first, second))
        ]
        return jnp.concatenate(rows, axis=0)

    own_up = up_rows(order_near, 0, upstream, pair_up)
    near_up = swapped(up_rows(order_near, 1, upstream, pair_up), 2)
    saved_1 = swapped(packed[1], 2)
    saved_2 = swapped(packed[2], 4)
    saved_3 = swapped(packed[3], 6)
    two_up = up_rows(order_far, 0, far_up, far_pair_up)
    three_up = swapped(up_rows(order_far, 1, far_up, far_pair_up), 2)

    def backward(up, pack):
        saved = pack[:, : 2 * units]
        gate = pack[:, 2 * units : 2 * units + 1].astype(f32)
        grad_hidden = lax.dot_general(up, w_down[0], LAST, preferred_element_type=f32)
        grad_a, grad_b, scaled = hidden_grads(grad_hidden, saved, gate)
        back = lax.dot_general(grad_a, w_gate[0], LAST, preferred_element_type=f32)
        back = back + lax.dot_general(grad_b, w_up[0], LAST, preferred_element_type=f32)
        return back.astype(bf16), scaled

    back_0, scaled_0 = backward(own_up, packed[0])
    back_1, scaled_1 = backward(near_up, saved_1)
    back_2, scaled_2 = backward(two_up, saved_2)
    back_3, scaled_3 = backward(three_up, saved_3)
    home_1 = swapped(back_1, 2)
    home_2 = swapped(back_2, 4)
    home_3 = swapped(back_3, 6)

    scaled = jnp.concatenate([scaled_0, scaled_1, scaled_2, scaled_3], axis=0)
    ups = jnp.concatenate([own_up, near_up, two_up, three_up], axis=0)
    down = lax.dot_general(scaled, ups, FIRST, preferred_element_type=f32).astype(bf16)

    home = jnp.stack([back_0, home_1, home_2, home_3]).reshape(4, 2, cap, width)
    sums = [
        lax.dot_general(
            order_near[n].astype(bf16).reshape(4 * cap, tokens),
            home[:, n].reshape(4 * cap, width),
            FIRST,
            preferred_element_type=f32,
        )
        for n in range(2)
    ]
    other = swapped(sums[1].astype(bf16), 1)
    total = (sums[0] + other.astype(f32)).astype(bf16)
    return shifted_2(total[None], "section", -1), down[None]


def on_device(*args):
    if lax.axis_size("expert") == EXPERTS:
        return on_device_pairs(*args)
    return on_device_general(*args)


def solution(mesh):
    placed = (
        P("section", "expert", None),
        P("section", "expert", None, None, None),
        P("section", "expert", None),
        P("section", "expert", None),
        P("section", None, "expert"),
        P("section", None, "expert"),
        P("section", "expert", None),
    )
    return jax.shard_map(
        on_device,
        mesh=mesh,
        in_specs=placed,
        out_specs=(P("section", "expert", None), P("section", "expert", None)),
        check_vma=False,
    )
```

```python
import jax
import jax.numpy as jnp
from jax import lax
from jax.experimental import pallas as pl
from jax.experimental.pallas import tpu as pltpu
from jax.sharding import PartitionSpec as P

EXPERTS = 8


def shifted_2(value, axis, steps):
    count = lax.axis_size(axis)
    pairs = [(source, (source + steps) % count) for source in range(count)]
    return lax.ppermute(value, axis, pairs)


def expert_rows(upstream, saved_rows, gate_rows, weight_gate, weight_up, weight_down):
    hid_units = weight_down.shape[0]
    grad_hidden = (
        lax.dot_general(
            upstream, weight_down, (((1,), (1,)), ((), ())), preferred_element_type=jnp.float32
        )
        * gate_rows[:, None]
    )
    saved_f = saved_rows.astype(jnp.float32)
    gate_pre = saved_f[:, :hid_units]
    up_pre = saved_f[:, hid_units:]
    sigmoid_g = jax.nn.sigmoid(gate_pre)
    silu_val = gate_pre * sigmoid_g
    grad_gate = (grad_hidden * up_pre * sigmoid_g * (1.0 + gate_pre * (1.0 - sigmoid_g))).astype(
        jnp.bfloat16
    )
    grad_upper = (grad_hidden * silu_val).astype(jnp.bfloat16)
    scaled_hidden = (gate_rows[:, None] * silu_val * up_pre).astype(jnp.bfloat16)
    contract_last = (((1,), (1,)), ((), ()))
    back_rows = lax.dot_general(
        grad_gate, weight_gate, contract_last, preferred_element_type=jnp.float32
    )
    back_rows = (
        back_rows
        + lax.dot_general(grad_upper, weight_up, contract_last, preferred_element_type=jnp.float32)
    ).astype(jnp.bfloat16)
    weight_term = lax.dot_general(
        scaled_hidden, upstream, (((0,), (0,)), ((), ())), preferred_element_type=jnp.float32
    )
    return (back_rows, weight_term)


def on_device_general(grad_out, pre_act, route_ids, route_gate, w_gate, w_up, w_down):
    member_count = lax.axis_size("expert")
    group_size = member_count // EXPERTS
    token_count = grad_out.shape[1]
    model_width = grad_out.shape[2]
    hid_units = w_down.shape[1]
    slot_cap = 3 * token_count // 8
    part_rows = slot_cap // group_size
    upstream = grad_out[0]
    route_rows = route_ids[0]
    gate_vals = route_gate[0]
    saved_acts = pre_act[0]
    weight_gate = w_gate[0]
    weight_up = w_up[0]
    weight_down = w_down[0]
    picked = route_rows[:, :, None] == jnp.arange(EXPERTS, dtype=jnp.int32)[None, None, :]
    is_named = jnp.any(picked, axis=1).astype(jnp.int32)
    slot_rank = jnp.cumsum(is_named, axis=0) - 1
    slot_index = jnp.where(is_named > 0, slot_rank, -1)
    selector = slot_index.T[:, None, :] == jnp.arange(slot_cap, dtype=jnp.int32)[None, :, None]
    order_sel = selector.reshape(EXPERTS, group_size, part_rows, token_count).transpose(1, 0, 2, 3)
    order_bf = order_sel.astype(jnp.bfloat16)
    gate_sel = jnp.sum(jnp.where(picked, gate_vals[:, :, None].astype(jnp.float32), 0.0), axis=1)
    saved_sel = jnp.zeros((token_count, EXPERTS, 2, saved_acts.shape[3]), jnp.bfloat16)
    for pick_index in range(saved_acts.shape[1]):
        saved_sel = jnp.where(
            picked[:, pick_index, :, None, None], saved_acts[:, pick_index, None, :, :], saved_sel
        )
    saved_rows = jnp.einsum(
        "gect,tex->gecx",
        order_bf,
        saved_sel.reshape(token_count, EXPERTS, -1),
        preferred_element_type=jnp.float32,
    ).astype(jnp.bfloat16)
    saved_rows = saved_rows.reshape(
        group_size, EXPERTS, part_rows, 2, group_size, hid_units
    ).transpose(0, 1, 4, 2, 3, 5)
    saved_buf = saved_rows.reshape(group_size, member_count, part_rows, 2 * hid_units)
    gate_rows = jnp.einsum("gect,te->gec", order_sel.astype(jnp.float32), gate_sel).astype(
        jnp.bfloat16
    )
    gate_buf = jnp.broadcast_to(
        gate_rows[:, :, None, :], (group_size, EXPERTS, group_size, part_rows)
    ).reshape(group_size, member_count, part_rows)
    upstream_rows = jnp.dot(
        order_bf.reshape(-1, token_count), upstream, preferred_element_type=jnp.float32
    ).astype(jnp.bfloat16)
    upstream_rows = upstream_rows.reshape(group_size, EXPERTS, 1, part_rows, model_width)
    upstream_buf = jnp.broadcast_to(
        upstream_rows, (group_size, EXPERTS, group_size, part_rows, model_width)
    )
    upstream_buf = upstream_buf.reshape(group_size, member_count, part_rows, model_width)
    recv_up, recv_saved, recv_gate = (
        lax.all_to_all(upstream_buf, "expert", split_axis=1, concat_axis=1, tiled=True),
        lax.all_to_all(saved_buf, "expert", split_axis=1, concat_axis=1, tiled=True),
        lax.all_to_all(gate_buf, "expert", split_axis=1, concat_axis=1, tiled=True),
    )
    up_flat = recv_up.reshape(-1, model_width)
    saved_flat = recv_saved.reshape(-1, 2 * hid_units)
    gate_flat = recv_gate.reshape(-1)
    gate_f = gate_flat.astype(jnp.float32)
    back_rows, down_sum = expert_rows(
        up_flat, saved_flat, gate_f, weight_gate, weight_up, weight_down
    )
    back_buf = back_rows.reshape(group_size, member_count, part_rows, model_width)
    returned = lax.all_to_all(back_buf, "expert", split_axis=1, concat_axis=1, tiled=True)
    member_sum = (
        returned.astype(jnp.float32)
        .reshape(group_size, EXPERTS, group_size, part_rows, model_width)
        .sum(axis=2)
    )
    summed = lax.optimization_barrier(member_sum.astype(jnp.bfloat16)).astype(jnp.float32)
    token_grad = lax.dot_general(
        order_sel.astype(jnp.float32).reshape(-1, token_count),
        summed.reshape(-1, model_width),
        (((0,), (0,)), ((), ())),
        precision=lax.Precision.HIGHEST,
        preferred_element_type=jnp.float32,
    )
    shifted = shifted_2(token_grad.astype(jnp.bfloat16)[None], "section", -1)
    return (shifted, down_sum.astype(jnp.bfloat16)[None])


LAST = (((1,), (1,)), ((), ()))
FIRST = (((0,), (0,)), ((), ()))
F32 = jnp.float32
BF16 = jnp.bfloat16
GATE_LANES = 128


def swapped(value, mask):
    count = lax.axis_size("expert")
    return lax.ppermute(value, "expert", [(i, i ^ mask) for i in range(count)])


def slot_order(own_meta, pair_meta, experts, cap):
    lanes = own_meta.shape[1]
    lane = lax.broadcasted_iota(jnp.int32, (8, lanes), 1)
    first = lane < lanes // 2
    packed = jnp.where(first, own_meta[...], pair_meta[...])
    ids = jnp.right_shift(packed.astype(jnp.int32), 1)
    gates = packed - 2.0 * ids.astype(F32)
    row = lax.broadcasted_iota(jnp.int32, (8, lanes), 0)
    wanted = jnp.bitwise_xor(lax.axis_index("expert"), 2 * row)
    hit_0 = ids[0:1] == wanted
    hit_1 = ids[1:2] == wanted
    named = jnp.where(jnp.logical_or(hit_0, hit_1), 1.0, 0.0)
    gate = jnp.where(hit_0, gates[0:1], jnp.where(hit_1, gates[1:2], 0.0))
    before = lax.broadcasted_iota(jnp.int32, (lanes, lanes), 0)
    after = lax.broadcasted_iota(jnp.int32, (lanes, lanes), 1)
    half = lanes // 2
    same = (before < half) == (after < half)
    upto = jnp.where(jnp.logical_and(before <= after, same), 1.0, 0.0).astype(BF16)
    counts = jnp.dot(named.astype(BF16), upto, preferred_element_type=F32)
    slots = jnp.where(named > 0.5, counts.astype(jnp.int32) - 1, -1)
    slot_no = lax.broadcasted_iota(jnp.int32, (cap, lanes), 0)
    in_first = lax.broadcasted_iota(jnp.int32, (cap, lanes), 1) < half
    rows = []
    for e in range(experts):
        match = jnp.where(slots[e : e + 1] == slot_no, 1.0, 0.0)
        rows.append(jnp.where(in_first, match, 0.0))
        rows.append(jnp.where(in_first, 0.0, match))
    return rows, jnp.where(hit_0, 1.0, 0.0), jnp.where(hit_1, 1.0, 0.0), gate


def near_kernel(
    own_meta, pair_meta, own_up, pair_up, own_saved, pair_saved,
    up_0, up_1, pack_0, pack_1, pack_2, pack_3, order_out,
):
    cap = up_0.shape[0] // 2
    wide = own_saved.shape[2]
    rows, hit_0, hit_1, gate = slot_order(own_meta, pair_meta, 4, cap)
    order = jnp.concatenate(rows, axis=0)
    order_bf = order.astype(BF16)
    order_out[...] = order_bf
    ups = jnp.concatenate([own_up[...], pair_up[...]], axis=0)
    picked = jnp.dot(order_bf[: 4 * cap], ups, preferred_element_type=F32)
    up_0[...] = picked[: 2 * cap].astype(BF16)
    up_1[...] = picked[2 * cap :].astype(BF16)
    sel_0 = jnp.concatenate([rows[n] * hit_0[n // 2 : n // 2 + 1] for n in range(8)], axis=0)
    sel_1 = jnp.concatenate([rows[n] * hit_1[n // 2 : n // 2 + 1] for n in range(8)], axis=0)
    sel = jnp.concatenate([sel_0.astype(BF16), sel_1.astype(BF16)], axis=1)
    saved = jnp.concatenate([own_saved[0], pair_saved[0], own_saved[1], pair_saved[1]], axis=0)
    got = jnp.dot(sel, saved, preferred_element_type=F32)
    gate_rows = jnp.concatenate(
        [jnp.sum(rows[n] * gate[n // 2 : n // 2 + 1], axis=1, keepdims=True) for n in range(8)],
        axis=0,
    )
    gate_cols = jnp.broadcast_to(gate_rows, (8 * cap, GATE_LANES))
    for n, pack in enumerate((pack_0, pack_1, pack_2, pack_3)):
        part = slice(2 * cap * n, 2 * cap * (n + 1))
        pack[:, :wide] = got[part].astype(BF16)
        pack[:, wide:] = gate_cols[part].astype(BF16)


def far_kernel(own_meta, pair_meta, own_up, pair_up, up_2, up_3):
    cap = up_2.shape[0] // 2
    rows = slot_order(own_meta, pair_meta, 2, cap)[0]
    order = jnp.concatenate(rows, axis=0).astype(BF16)
    ups = jnp.concatenate([own_up[...], pair_up[...]], axis=0)
    picked = jnp.dot(order, ups, preferred_element_type=F32)
    up_2[...] = picked[: 2 * cap].astype(BF16)
    up_3[...] = picked[2 * cap :].astype(BF16)


def local_call(kernel, outs, args, flops):
    moved = sum(a.size * a.dtype.itemsize for a in args)
    moved += sum(o.size * o.dtype.itemsize for o in outs)
    whole = pl.BlockSpec(memory_space=pltpu.VMEM)
    return pl.pallas_call(
        kernel,
        out_shape=outs,
        in_specs=[whole] * len(args),
        out_specs=[whole] * len(outs),
        compiler_params=pltpu.CompilerParams(vmem_limit_bytes=24 * 1024 * 1024),
        cost_estimate=pl.CostEstimate(flops=flops, bytes_accessed=moved, transcendentals=0),
    )(*args)


def hidden_grads(grad_hidden, saved, gate):
    units = grad_hidden.shape[1]
    saved_f = saved.astype(F32)
    gate_pre = saved_f[:, :units]
    up_pre = saved_f[:, units:]
    sig = jax.nn.sigmoid(gate_pre)
    silu = gate_pre * sig
    grad_h = grad_hidden * gate
    grad_a = (grad_h * up_pre * sig * (1.0 + gate_pre * (1.0 - sig))).astype(BF16)
    grad_b = (grad_h * silu).astype(BF16)
    scaled = (gate * silu * up_pre).astype(BF16)
    return grad_a, grad_b, scaled


def on_device_pairs(grad_out, pre_act, route_ids, route_gate, w_gate, w_up, w_down):
    tokens, width = grad_out.shape[1:]
    units = w_down.shape[1]
    wide = 2 * units
    cap = 3 * tokens // 8
    upstream = grad_out[0]

    meta = (2 * route_ids[0]).astype(F32) + route_gate[0].astype(F32)
    meta = jnp.concatenate([meta.T, meta.T], axis=1)
    meta = jnp.pad(meta, ((0, 8 - meta.shape[0]), (0, 0)))
    saved_all = pre_act[0].transpose(1, 0, 2, 3).reshape(-1, tokens, wide)

    far_up = swapped(upstream, 4)
    far_meta = swapped(meta, 4)
    pair_up = swapped(upstream, 1)
    pair_meta = swapped(meta, 1)
    pair_saved = swapped(saved_all, 1)
    far_pair_up = swapped(far_up, 1)
    far_pair_meta = swapped(far_meta, 1)

    up_shape = jax.ShapeDtypeStruct((2 * cap, width), BF16)
    pack_shape = jax.ShapeDtypeStruct((2 * cap, wide + GATE_LANES), BF16)
    order_shape = jax.ShapeDtypeStruct((8 * cap, 2 * tokens), BF16)
    own_rows, near_rows, pack_0, pack_1, pack_2, pack_3, order = local_call(
        near_kernel,
        [up_shape] * 2 + [pack_shape] * 4 + [order_shape],
        (meta, pair_meta, upstream, pair_up, saved_all, pair_saved),
        2 * 8 * cap * 4 * tokens * (width + wide),
    )
    near_rows = swapped(near_rows, 2)
    pack_2 = swapped(pack_2, 4)
    pack_3 = swapped(pack_3, 6)
    pack_1 = swapped(pack_1, 2)
    two_rows, three_rows = local_call(
        far_kernel,
        [up_shape] * 2,
        (far_meta, far_pair_meta, far_up, far_pair_up),
        2 * 4 * cap * 2 * tokens * width,
    )
    three_rows = swapped(three_rows, 2)

    def backward(up, pack):
        saved = pack[:, :wide]
        gate = pack[:, wide : wide + 1].astype(F32)
        grad_hidden = lax.dot_general(up, w_down[0], LAST, preferred_element_type=F32)
        grad_a, grad_b, scaled = hidden_grads(grad_hidden, saved, gate)
        back = lax.dot_general(grad_a, w_gate[0], LAST, preferred_element_type=F32)
        back = back + lax.dot_general(grad_b, w_up[0], LAST, preferred_element_type=F32)
        return back.astype(BF16), scaled

    close_up = jnp.concatenate([own_rows, near_rows], axis=0)
    back_close, scaled_close = backward(close_up, jnp.concatenate([pack_0, pack_1], axis=0))
    back_2, scaled_2 = backward(two_rows, pack_2)
    back_3, scaled_3 = backward(three_rows, pack_3)
    home_2 = swapped(back_2, 4)
    home_3 = swapped(back_3, 6)
    home_1 = swapped(back_close[2 * cap :], 2)

    scaled = jnp.concatenate([scaled_close, scaled_2, scaled_3], axis=0)
    ups = jnp.concatenate([close_up, two_rows, three_rows], axis=0)
    down = lax.dot_general(scaled, ups, FIRST, preferred_element_type=F32).astype(BF16)

    home = jnp.concatenate([back_close[: 2 * cap], home_1, home_2, home_3], axis=0)
    sums = lax.dot_general(order, home, FIRST, preferred_element_type=F32)
    other = swapped(sums[tokens:].astype(BF16), 1)
    total = (sums[:tokens] + other.astype(F32)).astype(BF16)
    return shifted_2(total[None], "section", -1), down[None]


def on_device(*args):
    if lax.axis_size("expert") == EXPERTS:
        return on_device_pairs(*args)
    return on_device_general(*args)


def solution(mesh):
    placed = (
        P("section", "expert", None),
        P("section", "expert", None, None, None),
        P("section", "expert", None),
        P("section", "expert", None),
        P("section", None, "expert"),
        P("section", None, "expert"),
        P("section", "expert", None),
    )
    return jax.shard_map(
        on_device,
        mesh=mesh,
        in_specs=placed,
        out_specs=(P("section", "expert", None), P("section", "expert", None)),
        check_vma=False,
    )
```

```python
import functools

import jax
import jax.numpy as jnp
from jax import lax
from jax.experimental import pallas as pl
from jax.experimental.pallas import tpu as pltpu
from jax.sharding import PartitionSpec as P

EXPERTS = 8


def shifted_2(value, axis, steps):
    count = lax.axis_size(axis)
    pairs = [(source, (source + steps) % count) for source in range(count)]
    return lax.ppermute(value, axis, pairs)


def expert_rows(upstream, saved_rows, gate_rows, weight_gate, weight_up, weight_down):
    hid_units = weight_down.shape[0]
    grad_hidden = (
        lax.dot_general(
            upstream, weight_down, (((1,), (1,)), ((), ())), preferred_element_type=jnp.float32
        )
        * gate_rows[:, None]
    )
    saved_f = saved_rows.astype(jnp.float32)
    gate_pre = saved_f[:, :hid_units]
    up_pre = saved_f[:, hid_units:]
    sigmoid_g = jax.nn.sigmoid(gate_pre)
    silu_val = gate_pre * sigmoid_g
    grad_gate = (grad_hidden * up_pre * sigmoid_g * (1.0 + gate_pre * (1.0 - sigmoid_g))).astype(
        jnp.bfloat16
    )
    grad_upper = (grad_hidden * silu_val).astype(jnp.bfloat16)
    scaled_hidden = (gate_rows[:, None] * silu_val * up_pre).astype(jnp.bfloat16)
    contract_last = (((1,), (1,)), ((), ()))
    back_rows = lax.dot_general(
        grad_gate, weight_gate, contract_last, preferred_element_type=jnp.float32
    )
    back_rows = (
        back_rows
        + lax.dot_general(grad_upper, weight_up, contract_last, preferred_element_type=jnp.float32)
    ).astype(jnp.bfloat16)
    weight_term = lax.dot_general(
        scaled_hidden, upstream, (((0,), (0,)), ((), ())), preferred_element_type=jnp.float32
    )
    return (back_rows, weight_term)


def on_device_general(grad_out, pre_act, route_ids, route_gate, w_gate, w_up, w_down):
    member_count = lax.axis_size("expert")
    group_size = member_count // EXPERTS
    token_count = grad_out.shape[1]
    model_width = grad_out.shape[2]
    hid_units = w_down.shape[1]
    slot_cap = 3 * token_count // 8
    part_rows = slot_cap // group_size
    upstream = grad_out[0]
    route_rows = route_ids[0]
    gate_vals = route_gate[0]
    saved_acts = pre_act[0]
    weight_gate = w_gate[0]
    weight_up = w_up[0]
    weight_down = w_down[0]
    picked = route_rows[:, :, None] == jnp.arange(EXPERTS, dtype=jnp.int32)[None, None, :]
    is_named = jnp.any(picked, axis=1).astype(jnp.int32)
    slot_rank = jnp.cumsum(is_named, axis=0) - 1
    slot_index = jnp.where(is_named > 0, slot_rank, -1)
    selector = slot_index.T[:, None, :] == jnp.arange(slot_cap, dtype=jnp.int32)[None, :, None]
    order_sel = selector.reshape(EXPERTS, group_size, part_rows, token_count).transpose(1, 0, 2, 3)
    order_bf = order_sel.astype(jnp.bfloat16)
    gate_sel = jnp.sum(jnp.where(picked, gate_vals[:, :, None].astype(jnp.float32), 0.0), axis=1)
    saved_sel = jnp.zeros((token_count, EXPERTS, 2, saved_acts.shape[3]), jnp.bfloat16)
    for pick_index in range(saved_acts.shape[1]):
        saved_sel = jnp.where(
            picked[:, pick_index, :, None, None], saved_acts[:, pick_index, None, :, :], saved_sel
        )
    saved_rows = jnp.einsum(
        "gect,tex->gecx",
        order_bf,
        saved_sel.reshape(token_count, EXPERTS, -1),
        preferred_element_type=jnp.float32,
    ).astype(jnp.bfloat16)
    saved_rows = saved_rows.reshape(
        group_size, EXPERTS, part_rows, 2, group_size, hid_units
    ).transpose(0, 1, 4, 2, 3, 5)
    saved_buf = saved_rows.reshape(group_size, member_count, part_rows, 2 * hid_units)
    gate_rows = jnp.einsum("gect,te->gec", order_sel.astype(jnp.float32), gate_sel).astype(
        jnp.bfloat16
    )
    gate_buf = jnp.broadcast_to(
        gate_rows[:, :, None, :], (group_size, EXPERTS, group_size, part_rows)
    ).reshape(group_size, member_count, part_rows)
    upstream_rows = jnp.dot(
        order_bf.reshape(-1, token_count), upstream, preferred_element_type=jnp.float32
    ).astype(jnp.bfloat16)
    upstream_rows = upstream_rows.reshape(group_size, EXPERTS, 1, part_rows, model_width)
    upstream_buf = jnp.broadcast_to(
        upstream_rows, (group_size, EXPERTS, group_size, part_rows, model_width)
    )
    upstream_buf = upstream_buf.reshape(group_size, member_count, part_rows, model_width)
    recv_up, recv_saved, recv_gate = (
        lax.all_to_all(upstream_buf, "expert", split_axis=1, concat_axis=1, tiled=True),
        lax.all_to_all(saved_buf, "expert", split_axis=1, concat_axis=1, tiled=True),
        lax.all_to_all(gate_buf, "expert", split_axis=1, concat_axis=1, tiled=True),
    )
    up_flat = recv_up.reshape(-1, model_width)
    saved_flat = recv_saved.reshape(-1, 2 * hid_units)
    gate_flat = recv_gate.reshape(-1)
    gate_f = gate_flat.astype(jnp.float32)
    back_rows, down_sum = expert_rows(
        up_flat, saved_flat, gate_f, weight_gate, weight_up, weight_down
    )
    back_buf = back_rows.reshape(group_size, member_count, part_rows, model_width)
    returned = lax.all_to_all(back_buf, "expert", split_axis=1, concat_axis=1, tiled=True)
    member_sum = (
        returned.astype(jnp.float32)
        .reshape(group_size, EXPERTS, group_size, part_rows, model_width)
        .sum(axis=2)
    )
    summed = lax.optimization_barrier(member_sum.astype(jnp.bfloat16)).astype(jnp.float32)
    token_grad = lax.dot_general(
        order_sel.astype(jnp.float32).reshape(-1, token_count),
        summed.reshape(-1, model_width),
        (((0,), (0,)), ((), ())),
        precision=lax.Precision.HIGHEST,
        preferred_element_type=jnp.float32,
    )
    shifted = shifted_2(token_grad.astype(jnp.bfloat16)[None], "section", -1)
    return (shifted, down_sum.astype(jnp.bfloat16)[None])


LAST = (((1,), (1,)), ((), ()))
FIRST = (((0,), (0,)), ((), ()))
F32 = jnp.float32
BF16 = jnp.bfloat16
GATE_LANES = 128
SUM_COST = 8 * 1024 * 1024
OWN_LIMIT = 44


def swapped(value, mask):
    count = lax.axis_size("expert")
    return lax.ppermute(value, "expert", [(i, i ^ mask) for i in range(count)])


def slot_order(ids, gates, masks, cap):
    lanes = ids.shape[1]
    half = lanes // 2
    row = lax.broadcasted_iota(jnp.int32, (8, lanes), 0)
    wanted = jnp.full((8, lanes), masks[0], jnp.int32)
    for n in range(1, len(masks)):
        wanted = jnp.where(row == n, masks[n], wanted)
    wanted = jnp.bitwise_xor(lax.axis_index("expert"), wanted)
    hit_0 = ids[0:1] == wanted
    hit_1 = ids[1:2] == wanted
    named = jnp.where(jnp.logical_or(hit_0, hit_1), 1.0, 0.0)
    gate = jnp.where(hit_0, gates[0:1], jnp.where(hit_1, gates[1:2], 0.0))
    before = lax.broadcasted_iota(jnp.int32, (lanes, lanes), 0)
    after = lax.broadcasted_iota(jnp.int32, (lanes, lanes), 1)
    same = (before < half) == (after < half)
    upto = jnp.where(jnp.logical_and(before <= after, same), 1.0, 0.0).astype(BF16)
    counts = jnp.dot(named.astype(BF16), upto, preferred_element_type=F32)
    slots = jnp.where(named > 0.5, counts.astype(jnp.int32) - 1, -1)
    slot_no = lax.broadcasted_iota(jnp.int32, (cap, lanes), 0)
    in_first = lax.broadcasted_iota(jnp.int32, (cap, lanes), 1) < half
    rows = []
    for n in range(len(masks)):
        match = jnp.where(slots[n : n + 1] == slot_no, 1.0, 0.0)
        rows.append(jnp.where(in_first, match, 0.0))
        rows.append(jnp.where(in_first, 0.0, match))
    return rows, jnp.where(hit_0, 1.0, 0.0), jnp.where(hit_1, 1.0, 0.0), gate


def gate_columns(rows, gate):
    found = [
        jnp.sum(row * gate[n // 2 : n // 2 + 1], axis=1, keepdims=True)
        for n, row in enumerate(rows)
    ]
    found = jnp.concatenate(found, axis=0)
    return jnp.broadcast_to(found, (found.shape[0], GATE_LANES)).astype(BF16)


def near_kernel(
    own_ids, own_gate, own_up, own_act, pair_ids, pair_gate, pair_up, pair_act,
    routes, up_0, up_1, saved_0, saved_1, saved_2, saved_3, gate_0, acts,
):
    tokens = own_up.shape[0]
    cap, width = up_0.shape[0] // 2, up_0.shape[1]
    units = own_act.shape[3]
    wide = 2 * units
    ids = jnp.concatenate([own_ids[...], pair_ids[...]], axis=1)
    gates = jnp.concatenate([own_gate[...].astype(F32), pair_gate[...].astype(F32)], axis=1)
    picks = ids.shape[0]
    named = jnp.concatenate([ids.astype(F32), gates], axis=0)
    rest = jnp.zeros((routes.shape[0] - 2 * picks, routes.shape[1]), F32)
    named = jnp.concatenate([named, rest], axis=0)
    routes[...] = named.astype(BF16)
    saved_2[:, wide:] = named.astype(BF16)
    rows, hit_0, hit_1, gate = slot_order(ids, gates, (0, 2, 4, 6), cap)
    order_bf = jnp.concatenate(rows, axis=0).astype(BF16)
    gates = gate_columns(rows[:4], gate)
    gate_0[...] = gates[: 2 * cap]
    up_1[:, width:] = gates[2 * cap :]
    sel_0 = jnp.concatenate([rows[n] * hit_0[n // 2 : n // 2 + 1] for n in range(8)], axis=0)
    sel_1 = jnp.concatenate([rows[n] * hit_1[n // 2 : n // 2 + 1] for n in range(8)], axis=0)
    sel = jnp.concatenate([sel_0.astype(BF16), sel_1.astype(BF16)], axis=1)
    ups = jnp.concatenate([own_up[...], pair_up[...]], axis=0)
    picked = jnp.dot(order_bf[: 4 * cap], ups, preferred_element_type=F32)
    up_0[...] = picked[: 2 * cap].astype(BF16)
    up_1[:, :width] = picked[2 * cap :].astype(BF16)
    for block, act in enumerate((own_act, pair_act)):
        for pick in range(picks):
            low = (2 * pick + block) * tokens
            for side in range(2):
                part = act[:, pick, side, :]
                acts[low : low + tokens, side * units : (side + 1) * units] = part
    got = jnp.dot(sel, acts[...], preferred_element_type=F32)
    for n, out in enumerate((saved_0, saved_1, saved_2, saved_3)):
        out[:, :wide] = got[2 * cap * n : 2 * cap * (n + 1)].astype(BF16)


def read_routes(routes):
    named = routes.astype(F32)
    return named[:2].astype(jnp.int32), named[2:4]


def far_kernel(saved_2, both_up, up_2, up_3, gate_2):
    cap, width = up_2.shape[0] // 2, up_2.shape[1]
    tokens = both_up.shape[0] // 2
    ids, gates = read_routes(saved_2[:, saved_2.shape[1] - 2 * tokens :])
    rows, _, _, gate = slot_order(ids, gates, (0, 2), cap)
    order = jnp.concatenate(rows, axis=0)
    odd = lax.axis_index("expert") % 2 == 1
    order = jnp.where(odd, pltpu.roll(order, tokens, 1), order).astype(BF16)
    picked = jnp.dot(order, both_up[...], preferred_element_type=F32)
    gates = gate_columns(rows, gate)
    up_2[...] = picked[: 2 * cap].astype(BF16)
    up_3[:, :width] = picked[2 * cap :].astype(BF16)
    up_3[:, width:] = gates[2 * cap :]
    gate_2[...] = gates[: 2 * cap]


def through_expert(up, saved, gate, w_down, w_gate, w_up):
    grad_hidden = lax.dot_general(up, w_down[...], LAST, preferred_element_type=F32)
    grad_a, grad_b, scaled = hidden_grads(grad_hidden, saved, gate[:, :1].astype(F32))
    back = lax.dot_general(grad_a, w_gate[...], LAST, preferred_element_type=F32)
    back = back + lax.dot_general(grad_b, w_up[...], LAST, preferred_element_type=F32)
    return back.astype(BF16), scaled


def own_kernel(
    up, saved, gate, w_down, w_gate, w_up,
    back_out, scaled_out, down_here, gate_here, up_here, arrived,
):
    moves = ((w_down, down_here), (w_gate, gate_here), (w_up, up_here))
    copies = [pltpu.make_async_copy(a, b, arrived.at[n]) for n, (a, b) in enumerate(moves)]
    for copy in copies:
        copy.start()
    copies[0].wait()
    grad_hidden = lax.dot_general(up[...], down_here[...], LAST, preferred_element_type=F32)
    grad_a, grad_b, scaled = hidden_grads(grad_hidden, saved[...], gate[:, :1].astype(F32))
    scaled_out[...] = scaled
    copies[1].wait()
    back = lax.dot_general(grad_a, gate_here[...], LAST, preferred_element_type=F32)
    copies[2].wait()
    back = back + lax.dot_general(grad_b, up_here[...], LAST, preferred_element_type=F32)
    back_out[...] = back.astype(BF16)


def chunk_kernel(count, *refs):
    ups, saveds, gates = refs[:count], refs[count : 2 * count], refs[2 * count : 3 * count]
    w_down, w_gate, w_up = refs[3 * count : 3 * count + 3]
    backs, scaled_out = refs[3 * count + 3 : -1], refs[-1]
    width, units = w_gate.shape[0], w_gate.shape[1]
    each = ups[0].shape[0]
    up = jnp.concatenate([ref[:, :width] for ref in ups], axis=0)
    saved = jnp.concatenate([ref[:, : 2 * units] for ref in saveds], axis=0)
    gate = jnp.concatenate([ref[:, ref.shape[1] - GATE_LANES :] for ref in gates], axis=0)
    back, scaled_out[...] = through_expert(up, saved, gate, w_down, w_gate, w_up)
    for n, out in enumerate(backs):
        out[...] = back[n * each : (n + 1) * each]


def down_kernel(scaled_a, scaled_b, scaled_c, up_a, up_b, up_c, up_d, out):
    scaled = jnp.concatenate([scaled_a[...], scaled_b[...], scaled_c[...]], axis=0)
    ups = jnp.concatenate([up_a[...], up_b[...], up_c[...], up_d[...]], axis=0)
    out[...] = lax.dot_general(scaled, ups, FIRST, preferred_element_type=F32).astype(BF16)


def sum_kernel(routes, rows_0, rows_1, rows_2, own, other):
    tokens = own.shape[0]
    ids, gates = read_routes(routes[...])
    order = slot_order(ids, gates, (0, 2, 4), rows_0.shape[0] // 2)[0]
    order = jnp.concatenate(order, axis=0).astype(BF16)
    rows = jnp.concatenate([rows_0[...], rows_1[...], rows_2[...]], axis=0)
    back = lax.dot_general(order, rows, FIRST, preferred_element_type=F32)
    own[...] = back[:tokens]
    other[...] = back[tokens:].astype(BF16)


def last_kernel(routes, own, other, rows_6, rows_7, out):
    tokens, cap = own.shape[0], rows_6.shape[0] // 2
    ids, gates = read_routes(routes[...])
    order = slot_order(ids, gates, (6, 7), cap)[0]
    order = jnp.concatenate([order[0], order[2]], axis=0).astype(BF16)
    rows = [rows_6[...].astype(F32)[:cap], rows_7[...].astype(F32)[cap:]]
    rows = jnp.concatenate(rows, axis=0).astype(BF16)
    back = lax.dot_general(order, rows, FIRST, preferred_element_type=F32)
    out[...] = (own[...] + other[...].astype(F32) + back[:tokens]).astype(BF16)


def local_call(kernel, outs, args, scratch=(), cost=0, limit=28, **blocks):
    whole = pl.BlockSpec(memory_space=pltpu.VMEM)
    if not blocks:
        blocks["in_specs"] = [whole] * len(args)
        blocks["out_specs"] = [whole] * len(outs)
    return pl.pallas_call(
        kernel,
        out_shape=outs,
        scratch_shapes=scratch,
        compiler_params=pltpu.CompilerParams(vmem_limit_bytes=limit * 1024 * 1024),
        cost_estimate=pl.CostEstimate(flops=0, bytes_accessed=cost, transcendentals=0),
        **blocks,
    )(*args)


def hidden_grads(grad_hidden, saved, gate):
    units = grad_hidden.shape[1]
    saved_f = saved.astype(F32)
    gate_pre = saved_f[:, :units]
    up_pre = saved_f[:, units:]
    sig = 1.0 / (1.0 + jnp.exp(-gate_pre))
    silu = gate_pre * sig
    grad_h = grad_hidden * gate
    grad_a = (grad_h * up_pre * sig * (1.0 + gate_pre * (1.0 - sig))).astype(BF16)
    grad_b = (grad_h * silu).astype(BF16)
    scaled = (gate * silu * up_pre).astype(BF16)
    return grad_a, grad_b, scaled


def after(value, *others):
    return lax.optimization_barrier((value,) + others)[0]


def before_section(value, mask):
    sections, count = lax.axis_size("section"), lax.axis_size("expert")
    pairs = [
        (s * count + e, (s + sections - 1) % sections * count + (e ^ mask))
        for s in range(sections)
        for e in range(count)
    ]
    return lax.ppermute(value, ("section", "expert"), pairs)


def on_device_pairs(grad_out, pre_act, route_ids, route_gate, w_gate, w_up, w_down):
    tokens, width = grad_out.shape[1:]
    units = w_down.shape[1]
    wide = 2 * units
    cap = 3 * tokens // 8
    upstream = grad_out[0]

    def shape(rows, lanes):
        return jax.ShapeDtypeStruct((rows, lanes), BF16)

    up, act = grad_out[0], pre_act[0]
    ids, gate = route_ids[0].T, route_gate[0].T
    far_up = swapped(up, 4)
    routes, own_rows, near_rows, saved_0, saved_1, saved_2, saved_3, gate_0 = local_call(
        near_kernel,
        [shape(2 * cap, 2 * tokens)]
        + [shape(2 * cap, width), shape(2 * cap, width + GATE_LANES)]
        + [shape(2 * cap, wide + (2 * tokens if n == 2 else 0)) for n in range(4)]
        + [shape(2 * cap, GATE_LANES)],
        (ids, gate, up, act, swapped(ids, 1), swapped(gate, 1), swapped(up, 1), swapped(act, 1)),
        [pltpu.VMEM((4 * tokens, wide), BF16)],
    )
    near_rows = swapped(near_rows, 2)
    saved_2 = swapped(saved_2, 4)
    saved_1 = swapped(saved_1, 2)
    vmem, hbm = (pl.BlockSpec(memory_space=space) for space in (pltpu.VMEM, pltpu.HBM))
    weights = (w_down[0], w_gate[0], w_up[0])
    back_0, scaled_0, *weights = local_call(
        own_kernel,
        [shape(2 * cap, width), shape(2 * cap, units)] + [shape(*w.shape) for w in weights],
        (own_rows, saved_0, gate_0, *weights),
        [pltpu.SemaphoreType.DMA((3,))],
        limit=OWN_LIMIT,
        in_specs=[vmem] * 3 + [hbm] * 3,
        out_specs=[vmem] * 5,
    )
    next_routes = before_section(routes, 0)
    far_up = after(far_up, back_0, next_routes)
    far_both = lax.all_gather(
        far_up, "expert", axis=0, tiled=True, axis_index_groups=[[i, i + 1] for i in range(0, 8, 2)]
    )
    saved_3 = swapped(after(saved_3, far_up), 6)
    two_rows, three_rows, gate_2 = local_call(
        far_kernel,
        [shape(2 * cap, width), shape(2 * cap, width + GATE_LANES), shape(2 * cap, GATE_LANES)],
        (saved_2, far_both),
    )
    three_rows = swapped(three_rows, 2)
    home_0 = before_section(back_0, 0)
    saved_1 = after(saved_1, two_rows)
    back_1, back_2, scaled_12 = local_call(
        functools.partial(chunk_kernel, 2),
        [shape(2 * cap, width)] * 2 + [shape(4 * cap, units)],
        (near_rows, two_rows, saved_1, saved_2, near_rows, gate_2, *weights),
    )
    saved_3 = after(saved_3, back_2, home_0)
    back_3, scaled_3 = local_call(
        functools.partial(chunk_kernel, 1),
        [shape(2 * cap, width), shape(2 * cap, units)],
        (three_rows, saved_3, three_rows, *weights),
    )
    home_2 = before_section(back_2, 4)
    home_1 = before_section(back_1, 2)
    home_3 = before_section(back_3, 6)
    parts = 4

    def columns(array):
        return pl.BlockSpec((array.shape[0], width // parts), lambda n: (0, n))

    def every(array):
        return pl.BlockSpec(array.shape, lambda n: (0, 0))

    scaled = (scaled_0, scaled_12, scaled_3)
    ups = (own_rows, near_rows, two_rows, three_rows)
    (down,) = local_call(
        down_kernel,
        [shape(units, width)],
        scaled + ups,
        grid=(parts,),
        in_specs=[every(a) for a in scaled] + [columns(a) for a in ups],
        out_specs=[pl.BlockSpec((units, width // parts), lambda n: (0, n))],
    )
    home_2 = after(home_2, down)
    summed, other = local_call(
        sum_kernel,
        [jax.ShapeDtypeStruct((tokens, width), F32), shape(tokens, width)],
        (next_routes, home_0, home_1, home_2),
        cost=SUM_COST,
    )
    other = swapped(other, 1)
    home_3 = after(home_3, summed)
    (total,) = local_call(
        last_kernel,
        [shape(tokens, width)],
        (next_routes, summed, other, home_3, swapped(home_3, 1)),
    )
    return total[None], down[None]


def on_device(*args):
    if lax.axis_size("expert") == EXPERTS:
        return on_device_pairs(*args)
    return on_device_general(*args)


def solution(mesh):
    placed = (
        P("section", "expert", None),
        P("section", "expert", None, None, None),
        P("section", "expert", None),
        P("section", "expert", None),
        P("section", None, "expert"),
        P("section", None, "expert"),
        P("section", "expert", None),
    )
    return jax.shard_map(
        on_device,
        mesh=mesh,
        in_specs=placed,
        out_specs=(P("section", "expert", None), P("section", "expert", None)),
        check_vma=False,
    )
```

```python
import jax
import jax.numpy as jnp
from jax import lax
from jax.experimental import pallas as pl
from jax.experimental.pallas import tpu as pltpu
from jax.sharding import PartitionSpec as P

EXPERTS = 8


def shifted_2(value, axis, steps):
    count = lax.axis_size(axis)
    pairs = [(source, (source + steps) % count) for source in range(count)]
    return lax.ppermute(value, axis, pairs)


def expert_rows(upstream, saved_rows, gate_rows, weight_gate, weight_up, weight_down):
    hid_units = weight_down.shape[0]
    grad_hidden = (
        lax.dot_general(
            upstream, weight_down, (((1,), (1,)), ((), ())), preferred_element_type=jnp.float32
        )
        * gate_rows[:, None]
    )
    saved_f = saved_rows.astype(jnp.float32)
    gate_pre = saved_f[:, :hid_units]
    up_pre = saved_f[:, hid_units:]
    sigmoid_g = jax.nn.sigmoid(gate_pre)
    silu_val = gate_pre * sigmoid_g
    grad_gate = (grad_hidden * up_pre * sigmoid_g * (1.0 + gate_pre * (1.0 - sigmoid_g))).astype(
        jnp.bfloat16
    )
    grad_upper = (grad_hidden * silu_val).astype(jnp.bfloat16)
    scaled_hidden = (gate_rows[:, None] * silu_val * up_pre).astype(jnp.bfloat16)
    contract_last = (((1,), (1,)), ((), ()))
    back_rows = lax.dot_general(
        grad_gate, weight_gate, contract_last, preferred_element_type=jnp.float32
    )
    back_rows = (
        back_rows
        + lax.dot_general(grad_upper, weight_up, contract_last, preferred_element_type=jnp.float32)
    ).astype(jnp.bfloat16)
    weight_term = lax.dot_general(
        scaled_hidden, upstream, (((0,), (0,)), ((), ())), preferred_element_type=jnp.float32
    )
    return (back_rows, weight_term)


def on_device_general(grad_out, pre_act, route_ids, route_gate, w_gate, w_up, w_down):
    member_count = lax.axis_size("expert")
    group_size = member_count // EXPERTS
    token_count = grad_out.shape[1]
    model_width = grad_out.shape[2]
    hid_units = w_down.shape[1]
    slot_cap = 3 * token_count // 8
    part_rows = slot_cap // group_size
    upstream = grad_out[0]
    route_rows = route_ids[0]
    gate_vals = route_gate[0]
    saved_acts = pre_act[0]
    weight_gate = w_gate[0]
    weight_up = w_up[0]
    weight_down = w_down[0]
    picked = route_rows[:, :, None] == jnp.arange(EXPERTS, dtype=jnp.int32)[None, None, :]
    is_named = jnp.any(picked, axis=1).astype(jnp.int32)
    slot_rank = jnp.cumsum(is_named, axis=0) - 1
    slot_index = jnp.where(is_named > 0, slot_rank, -1)
    selector = slot_index.T[:, None, :] == jnp.arange(slot_cap, dtype=jnp.int32)[None, :, None]
    order_sel = selector.reshape(EXPERTS, group_size, part_rows, token_count).transpose(1, 0, 2, 3)
    order_bf = order_sel.astype(jnp.bfloat16)
    gate_sel = jnp.sum(jnp.where(picked, gate_vals[:, :, None].astype(jnp.float32), 0.0), axis=1)
    saved_sel = jnp.zeros((token_count, EXPERTS, 2, saved_acts.shape[3]), jnp.bfloat16)
    for pick_index in range(saved_acts.shape[1]):
        saved_sel = jnp.where(
            picked[:, pick_index, :, None, None], saved_acts[:, pick_index, None, :, :], saved_sel
        )
    saved_rows = jnp.einsum(
        "gect,tex->gecx",
        order_bf,
        saved_sel.reshape(token_count, EXPERTS, -1),
        preferred_element_type=jnp.float32,
    ).astype(jnp.bfloat16)
    saved_rows = saved_rows.reshape(
        group_size, EXPERTS, part_rows, 2, group_size, hid_units
    ).transpose(0, 1, 4, 2, 3, 5)
    saved_buf = saved_rows.reshape(group_size, member_count, part_rows, 2 * hid_units)
    gate_rows = jnp.einsum("gect,te->gec", order_sel.astype(jnp.float32), gate_sel).astype(
        jnp.bfloat16
    )
    gate_buf = jnp.broadcast_to(
        gate_rows[:, :, None, :], (group_size, EXPERTS, group_size, part_rows)
    ).reshape(group_size, member_count, part_rows)
    upstream_rows = jnp.dot(
        order_bf.reshape(-1, token_count), upstream, preferred_element_type=jnp.float32
    ).astype(jnp.bfloat16)
    upstream_rows = upstream_rows.reshape(group_size, EXPERTS, 1, part_rows, model_width)
    upstream_buf = jnp.broadcast_to(
        upstream_rows, (group_size, EXPERTS, group_size, part_rows, model_width)
    )
    upstream_buf = upstream_buf.reshape(group_size, member_count, part_rows, model_width)
    recv_up, recv_saved, recv_gate = (
        lax.all_to_all(upstream_buf, "expert", split_axis=1, concat_axis=1, tiled=True),
        lax.all_to_all(saved_buf, "expert", split_axis=1, concat_axis=1, tiled=True),
        lax.all_to_all(gate_buf, "expert", split_axis=1, concat_axis=1, tiled=True),
    )
    up_flat = recv_up.reshape(-1, model_width)
    saved_flat = recv_saved.reshape(-1, 2 * hid_units)
    gate_flat = recv_gate.reshape(-1)
    gate_f = gate_flat.astype(jnp.float32)
    back_rows, down_sum = expert_rows(
        up_flat, saved_flat, gate_f, weight_gate, weight_up, weight_down
    )
    back_buf = back_rows.reshape(group_size, member_count, part_rows, model_width)
    returned = lax.all_to_all(back_buf, "expert", split_axis=1, concat_axis=1, tiled=True)
    member_sum = (
        returned.astype(jnp.float32)
        .reshape(group_size, EXPERTS, group_size, part_rows, model_width)
        .sum(axis=2)
    )
    summed = lax.optimization_barrier(member_sum.astype(jnp.bfloat16)).astype(jnp.float32)
    token_grad = lax.dot_general(
        order_sel.astype(jnp.float32).reshape(-1, token_count),
        summed.reshape(-1, model_width),
        (((0,), (0,)), ((), ())),
        precision=lax.Precision.HIGHEST,
        preferred_element_type=jnp.float32,
    )
    shifted = shifted_2(token_grad.astype(jnp.bfloat16)[None], "section", -1)
    return (shifted, down_sum.astype(jnp.bfloat16)[None])


LAST = (((1,), (1,)), ((), ()))
FIRST = (((0,), (0,)), ((), ()))
F32 = jnp.float32
BF16 = jnp.bfloat16
GATE_LANES = 128
SUM_COST = 0
FACTORS_COST = 0
OWN_LIMIT = 44
K0_COST = 10 ** 10


def swapped(value, mask):
    count = lax.axis_size("expert")
    return lax.ppermute(value, "expert", [(i, i ^ mask) for i in range(count)])


def earlier_tokens(lanes):
    half = lanes // 2
    before = lax.broadcasted_iota(jnp.int32, (lanes, lanes), 0)
    after = lax.broadcasted_iota(jnp.int32, (lanes, lanes), 1)
    same = (before < half) == (after < half)
    return jnp.where(jnp.logical_and(before <= after, same), 1.0, 0.0).astype(BF16)


def earlier_kernel(out):
    out[...] = earlier_tokens(out.shape[0])


def slot_order(ids, gates, masks, cap, upto=None):
    lanes = ids.shape[1]
    half = lanes // 2
    row = lax.broadcasted_iota(jnp.int32, (8, lanes), 0)
    wanted = jnp.full((8, lanes), masks[0], jnp.int32)
    for n in range(1, len(masks)):
        wanted = jnp.where(row == n, masks[n], wanted)
    wanted = jnp.bitwise_xor(lax.axis_index("expert"), wanted)
    hit_0 = ids[0:1] == wanted
    hit_1 = ids[1:2] == wanted
    named = jnp.where(jnp.logical_or(hit_0, hit_1), 1.0, 0.0)
    gate = jnp.where(hit_0, gates[0:1], jnp.where(hit_1, gates[1:2], 0.0))
    if upto is None:
        upto = earlier_tokens(lanes)
    counts = jnp.dot(named.astype(BF16), upto, preferred_element_type=F32)
    slots = jnp.where(named > 0.5, counts.astype(jnp.int32) - 1, -1)
    slot_no = lax.broadcasted_iota(jnp.int32, (cap, lanes), 0)
    in_first = lax.broadcasted_iota(jnp.int32, (cap, lanes), 1) < half
    rows = []
    for n in range(len(masks)):
        match = jnp.where(slots[n : n + 1] == slot_no, 1.0, 0.0)
        rows.append(jnp.where(in_first, match, 0.0))
        rows.append(jnp.where(in_first, 0.0, match))
    return rows, jnp.where(hit_0, 1.0, 0.0), jnp.where(hit_1, 1.0, 0.0), gate


def gate_columns(rows, gate):
    found = [
        jnp.sum(row * gate[n // 2 : n // 2 + 1], axis=1, keepdims=True)
        for n, row in enumerate(rows)
    ]
    found = jnp.concatenate(found, axis=0)
    return jnp.broadcast_to(found, (found.shape[0], GATE_LANES)).astype(BF16)


def near_kernel(
    upto, own_ids, own_gate, own_up, own_act, pair_ids, pair_gate, pair_up, pair_act,
    up_0, near, saved_0, saved_2, saved_3, gate_0, acts,
):
    tokens = own_up.shape[0]
    cap, width = up_0.shape[0] // 2, up_0.shape[1]
    units = own_act.shape[3]
    wide = 2 * units
    ids = jnp.concatenate([own_ids[...], pair_ids[...]], axis=1)
    gates = jnp.concatenate([own_gate[...].astype(F32), pair_gate[...].astype(F32)], axis=1)
    picks = ids.shape[0]
    named = jnp.concatenate([ids.astype(F32), gates], axis=0)
    rest = jnp.zeros((2 * cap - 2 * picks, ids.shape[1]), F32)
    named = jnp.concatenate([named, rest], axis=0)
    saved_2[:, wide:] = named.astype(BF16)
    rows, hit_0, hit_1, gate = slot_order(ids, gates, (0, 2, 4, 6), cap, upto[...])
    order_bf = jnp.concatenate(rows, axis=0).astype(BF16)
    gates = gate_columns(rows[:4], gate)
    gate_0[...] = gates[: 2 * cap]
    near[:, width : width + GATE_LANES] = gates[2 * cap :]
    sel_0 = jnp.concatenate([rows[n] * hit_0[n // 2 : n // 2 + 1] for n in range(8)], axis=0)
    sel_1 = jnp.concatenate([rows[n] * hit_1[n // 2 : n // 2 + 1] for n in range(8)], axis=0)
    sel = jnp.concatenate([sel_0.astype(BF16), sel_1.astype(BF16)], axis=1)
    ups = jnp.concatenate([own_up[...], pair_up[...]], axis=0)
    picked = jnp.dot(order_bf[: 4 * cap], ups, preferred_element_type=F32)
    up_0[...] = picked[: 2 * cap].astype(BF16)
    near[:, :width] = picked[2 * cap :].astype(BF16)
    for block, act in enumerate((own_act, pair_act)):
        for pick in range(picks):
            low = (2 * pick + block) * tokens
            for side in range(2):
                part = act[:, pick, side, :]
                acts[low : low + tokens, side * units : (side + 1) * units] = part
    got = jnp.dot(sel, acts[...], preferred_element_type=F32)
    low = near.shape[1] - wide
    for n, (out, lane) in enumerate(((saved_0, 0), (near, low), (saved_2, 0), (saved_3, 0))):
        out[:, lane : lane + wide] = got[2 * cap * n : 2 * cap * (n + 1)].astype(BF16)


def read_routes(routes):
    named = routes.astype(F32)
    return named[:2].astype(jnp.int32), named[2:4]


def far_kernel(saved_2, both_up, up_2, up_3, gate_2):
    cap, width = up_2.shape[0] // 2, up_2.shape[1]
    tokens = both_up.shape[0] // 2
    ids, gates = read_routes(saved_2[:, saved_2.shape[1] - 2 * tokens :])
    rows, _, _, gate = slot_order(ids, gates, (0, 2), cap)
    order = jnp.concatenate(rows, axis=0)
    odd = lax.axis_index("expert") % 2 == 1
    order = jnp.where(odd, pltpu.roll(order, tokens, 1), order).astype(BF16)
    picked = jnp.dot(order, both_up[...], preferred_element_type=F32)
    gates = gate_columns(rows, gate)
    up_2[...] = picked[: 2 * cap].astype(BF16)
    up_3[:, :width] = picked[2 * cap :].astype(BF16)
    up_3[:, width:] = gates[2 * cap :]
    gate_2[...] = gates[: 2 * cap]


def through_expert(up, saved, gate, w_down, w_gate, w_up):
    units = w_down.shape[0]
    gate = gate[:, :1].astype(F32)
    by_a, by_b, both = factors(saved[:, :units], saved[:, units:])
    grad_h = lax.dot_general(up, w_down[...], LAST, preferred_element_type=F32) * gate
    grad_a = (grad_h * by_a).astype(BF16)
    grad_b = (grad_h * by_b).astype(BF16)
    back = lax.dot_general(grad_a, w_gate[...], LAST, preferred_element_type=F32)
    back = back + lax.dot_general(grad_b, w_up[...], LAST, preferred_element_type=F32)
    return back.astype(BF16), (gate * both).astype(BF16)


def own_kernel(up, saved, gate, w_down, w_gate, w_up, back_out, scaled_out):
    back, scaled = through_expert(up[...], saved[...], gate[...], w_down, w_gate, w_up)
    back_out[...] = back
    scaled_out[...] = scaled


def both_kernel(near, up_2, saved_2, gate_2, w_down, w_gate, w_up, back_1, back_2, scaled_out):
    each, width = up_2.shape
    wide = 2 * w_down.shape[0]
    up = jnp.concatenate([near[:, :width], up_2[...]], axis=0)
    gate = jnp.concatenate([near[:, width : width + GATE_LANES], gate_2[...]], axis=0)
    saved = jnp.concatenate([near[:, width + GATE_LANES :], saved_2[:, :wide]], axis=0)
    back, scaled_out[...] = through_expert(up, saved, gate, w_down, w_gate, w_up)
    back_1[...] = back[:each]
    back_2[:, :width] = back[each:]
    back_2[:, width:] = saved_2[:, wide:]


def factors(gate_pre, up_pre):
    gate_pre, up_pre = gate_pre.astype(F32), up_pre.astype(F32)
    sig = 1.0 / (1.0 + jnp.exp(-gate_pre))
    silu = gate_pre * sig
    return up_pre * sig * (1.0 + gate_pre * (1.0 - sig)), silu, silu * up_pre


def factors_kernel(saved, by_a, by_b, both):
    units = by_a.shape[1]
    by_a[...], by_b[...], both[...] = factors(saved[:, :units], saved[:, units:])


def last_rows_kernel(up, by_a, by_b, both, w_down, w_gate, w_up, back_out, scaled_out):
    width = back_out.shape[1]
    gate = up[:, width : width + 1].astype(F32)
    grad_h = lax.dot_general(up[:, :width], w_down[...], LAST, preferred_element_type=F32) * gate
    grad_a = (grad_h * by_a[...]).astype(BF16)
    grad_b = (grad_h * by_b[...]).astype(BF16)
    scaled_out[...] = (gate * both[...]).astype(BF16)
    back = lax.dot_general(grad_a, w_gate[...], LAST, preferred_element_type=F32)
    back = back + lax.dot_general(grad_b, w_up[...], LAST, preferred_element_type=F32)
    back_out[...] = back.astype(BF16)


def down_kernel(scaled_a, scaled_b, scaled_c, up_a, up_b, up_c, up_d, out):
    scaled = jnp.concatenate([scaled_a[...], scaled_b[...], scaled_c[...]], axis=0)
    ups = jnp.concatenate([up_a[...], up_b[...], up_c[...], up_d[...]], axis=0)
    out[...] = lax.dot_general(scaled, ups, FIRST, preferred_element_type=F32).astype(BF16)


def two_sum_kernel(rows_1, rows_2, part, order_0, order_67):
    width = part.shape[1]
    ids, gates = read_routes(rows_2[:, width:])
    order = slot_order(ids, gates, (0, 2, 4, 6, 7), rows_2.shape[0] // 2)[0]
    order_0[...] = jnp.concatenate(order[:2], axis=0).astype(BF16)
    order_67[...] = jnp.concatenate([order[6], order[8]], axis=0).astype(BF16)
    order = jnp.concatenate(order[2:6], axis=0).astype(BF16)
    rows = jnp.concatenate([rows_1[...], rows_2[:, :width]], axis=0)
    part[...] = lax.dot_general(order, rows, FIRST, preferred_element_type=F32)


def sum_kernel(order, part, rows_0, own, other):
    tokens = own.shape[0]
    back = lax.dot_general(order[...], rows_0[...], FIRST, preferred_element_type=F32)
    back = part[...] + back
    own[...] = back[:tokens]
    other[...] = back[tokens:].astype(BF16)


def last_kernel(order, own, other, rows_6, rows_7, out):
    tokens, cap = own.shape[0], rows_6.shape[0] // 2
    rows = [rows_6[...].astype(F32)[:cap], rows_7[...].astype(F32)[cap:]]
    rows = jnp.concatenate(rows, axis=0).astype(BF16)
    back = lax.dot_general(order[...], rows, FIRST, preferred_element_type=F32)
    out[...] = (own[...] + other[...].astype(F32) + back[:tokens]).astype(BF16)


def local_call(kernel, outs, args, scratch=(), cost=0, limit=28, **blocks):
    whole = pl.BlockSpec(memory_space=pltpu.VMEM)
    if not blocks:
        blocks["in_specs"] = [whole] * len(args)
        blocks["out_specs"] = [whole] * len(outs)
    return pl.pallas_call(
        kernel,
        out_shape=outs,
        scratch_shapes=scratch,
        compiler_params=pltpu.CompilerParams(vmem_limit_bytes=limit * 1024 * 1024),
        cost_estimate=pl.CostEstimate(flops=cost, bytes_accessed=0, transcendentals=0),
        **blocks,
    )(*args)


def after(value, *others):
    return lax.optimization_barrier((value,) + others)[0]


def before_section(value, mask):
    sections, count = lax.axis_size("section"), lax.axis_size("expert")
    pairs = [
        (s * count + e, (s + sections - 1) % sections * count + (e ^ mask))
        for s in range(sections)
        for e in range(count)
    ]
    return lax.ppermute(value, ("section", "expert"), pairs)


def on_device_pairs(grad_out, pre_act, route_ids, route_gate, w_gate, w_up, w_down):
    tokens, width = grad_out.shape[1:]
    units = w_down.shape[1]
    wide = 2 * units
    cap = 3 * tokens // 8
    upstream = grad_out[0]

    def shape(rows, lanes):
        return jax.ShapeDtypeStruct((rows, lanes), BF16)

    up, act = grad_out[0], pre_act[0]
    ids, gate = route_ids[0].T, route_gate[0].T
    far_up = swapped(up, 4)
    (upto,) = local_call(earlier_kernel, [shape(2 * tokens, 2 * tokens)], (), cost=K0_COST)
    own_rows, near_rows, saved_0, saved_2, saved_3, gate_0 = local_call(
        near_kernel,
        [shape(2 * cap, width), shape(2 * cap, width + GATE_LANES + wide)]
        + [shape(2 * cap, wide), shape(2 * cap, wide + 2 * tokens), shape(2 * cap, wide)]
        + [shape(2 * cap, GATE_LANES)],
        (upto, ids, gate, up, act, swapped(ids, 1), swapped(gate, 1), swapped(up, 1), swapped(act, 1)),
        [pltpu.VMEM((4 * tokens, wide), BF16)],
    )
    near_rows = swapped(near_rows, 2)
    saved_2 = swapped(saved_2, 4)
    weights = (w_down[0], w_gate[0], w_up[0])
    back_0, scaled_0 = local_call(
        own_kernel,
        [shape(2 * cap, width), shape(2 * cap, units)],
        (own_rows, saved_0, gate_0, *weights),
    )
    far_up = after(far_up, back_0)
    far_both = lax.all_gather(
        far_up, "expert", axis=0, tiled=True, axis_index_groups=[[i, i + 1] for i in range(0, 8, 2)]
    )
    saved_3 = swapped(saved_3, 6)
    two_rows, three_rows, gate_2 = local_call(
        far_kernel,
        [shape(2 * cap, width), shape(2 * cap, width + GATE_LANES), shape(2 * cap, GATE_LANES)],
        (saved_2, far_both),
    )
    three_rows = swapped(three_rows, 2)
    home_0 = before_section(back_0, 0)
    near_rows = after(near_rows, home_0)
    back_1, back_2, scaled_12 = local_call(
        both_kernel,
        [shape(2 * cap, width), shape(2 * cap, width + 2 * tokens), shape(4 * cap, units)],
        (near_rows, two_rows, saved_2, gate_2, *weights),
    )
    saved_3 = after(saved_3, back_2)
    by_saved = local_call(
        factors_kernel,
        [jax.ShapeDtypeStruct((2 * cap, units), F32)] * 3,
        (saved_3,),
        cost=FACTORS_COST,
    )
    back_3, scaled_3 = local_call(
        last_rows_kernel,
        [shape(2 * cap, width), shape(2 * cap, units)],
        (three_rows, *by_saved, *weights),
    )
    home_2 = before_section(back_2, 4)
    home_1 = before_section(back_1, 2)
    home_3 = before_section(back_3, 6)
    parts = 4

    def columns(array):
        return pl.BlockSpec((array.shape[0], width // parts), lambda n: (0, n))

    def every(array):
        return pl.BlockSpec(array.shape, lambda n: (0, 0))

    scaled = (scaled_0, scaled_12, scaled_3)
    ups = (own_rows, near_rows, two_rows, three_rows)
    (down,) = local_call(
        down_kernel,
        [shape(units, width)],
        scaled + ups,
        grid=(parts,),
        in_specs=[every(a) for a in scaled] + [columns(a) for a in ups],
        out_specs=[pl.BlockSpec((units, width // parts), lambda n: (0, n))],
    )
    home_2 = after(home_2, down)
    part, order_0, order_67 = local_call(
        two_sum_kernel,
        [jax.ShapeDtypeStruct((2 * tokens, width), F32)]
        + [shape(2 * cap, 2 * tokens)] * 2,
        (home_1, home_2),
        cost=SUM_COST,
    )
    home_3 = after(home_3, part)
    summed, other = local_call(
        sum_kernel,
        [jax.ShapeDtypeStruct((tokens, width), F32), shape(tokens, width)],
        (order_0, part, home_0),
    )
    other = swapped(other, 1)
    (total,) = local_call(
        last_kernel,
        [shape(tokens, width)],
        (order_67, summed, other, home_3, swapped(home_3, 1)),
    )
    return total[None], down[None]


def on_device(*args):
    if lax.axis_size("expert") == EXPERTS:
        return on_device_pairs(*args)
    return on_device_general(*args)


def solution(mesh):
    placed = (
        P("section", "expert", None),
        P("section", "expert", None, None, None),
        P("section", "expert", None),
        P("section", "expert", None),
        P("section", None, "expert"),
        P("section", None, "expert"),
        P("section", "expert", None),
    )
    return jax.shard_map(
        on_device,
        mesh=mesh,
        in_specs=placed,
        out_specs=(P("section", "expert", None), P("section", "expert", None)),
        check_vma=False,
    )
```

```python
import jax
import jax.numpy as jnp
from jax import lax
from jax.experimental import pallas as pl
from jax.experimental.pallas import tpu as pltpu
from jax.sharding import PartitionSpec as P

EXPERTS = 8


def shifted_2(value, axis, steps):
    count = lax.axis_size(axis)
    pairs = [(source, (source + steps) % count) for source in range(count)]
    return lax.ppermute(value, axis, pairs)


def expert_rows(upstream, saved_rows, gate_rows, weight_gate, weight_up, weight_down):
    hid_units = weight_down.shape[0]
    grad_hidden = (
        lax.dot_general(
            upstream, weight_down, (((1,), (1,)), ((), ())), preferred_element_type=jnp.float32
        )
        * gate_rows[:, None]
    )
    saved_f = saved_rows.astype(jnp.float32)
    gate_pre = saved_f[:, :hid_units]
    up_pre = saved_f[:, hid_units:]
    sigmoid_g = jax.nn.sigmoid(gate_pre)
    silu_val = gate_pre * sigmoid_g
    grad_gate = (grad_hidden * up_pre * sigmoid_g * (1.0 + gate_pre * (1.0 - sigmoid_g))).astype(
        jnp.bfloat16
    )
    grad_upper = (grad_hidden * silu_val).astype(jnp.bfloat16)
    scaled_hidden = (gate_rows[:, None] * silu_val * up_pre).astype(jnp.bfloat16)
    contract_last = (((1,), (1,)), ((), ()))
    back_rows = lax.dot_general(
        grad_gate, weight_gate, contract_last, preferred_element_type=jnp.float32
    )
    back_rows = (
        back_rows
        + lax.dot_general(grad_upper, weight_up, contract_last, preferred_element_type=jnp.float32)
    ).astype(jnp.bfloat16)
    weight_term = lax.dot_general(
        scaled_hidden, upstream, (((0,), (0,)), ((), ())), preferred_element_type=jnp.float32
    )
    return (back_rows, weight_term)


def on_device_general(grad_out, pre_act, route_ids, route_gate, w_gate, w_up, w_down):
    member_count = lax.axis_size("expert")
    group_size = member_count // EXPERTS
    token_count = grad_out.shape[1]
    model_width = grad_out.shape[2]
    hid_units = w_down.shape[1]
    slot_cap = 3 * token_count // 8
    part_rows = slot_cap // group_size
    upstream = grad_out[0]
    route_rows = route_ids[0]
    gate_vals = route_gate[0]
    saved_acts = pre_act[0]
    weight_gate = w_gate[0]
    weight_up = w_up[0]
    weight_down = w_down[0]
    picked = route_rows[:, :, None] == jnp.arange(EXPERTS, dtype=jnp.int32)[None, None, :]
    is_named = jnp.any(picked, axis=1).astype(jnp.int32)
    slot_rank = jnp.cumsum(is_named, axis=0) - 1
    slot_index = jnp.where(is_named > 0, slot_rank, -1)
    selector = slot_index.T[:, None, :] == jnp.arange(slot_cap, dtype=jnp.int32)[None, :, None]
    order_sel = selector.reshape(EXPERTS, group_size, part_rows, token_count).transpose(1, 0, 2, 3)
    order_bf = order_sel.astype(jnp.bfloat16)
    gate_sel = jnp.sum(jnp.where(picked, gate_vals[:, :, None].astype(jnp.float32), 0.0), axis=1)
    saved_sel = jnp.zeros((token_count, EXPERTS, 2, saved_acts.shape[3]), jnp.bfloat16)
    for pick_index in range(saved_acts.shape[1]):
        saved_sel = jnp.where(
            picked[:, pick_index, :, None, None], saved_acts[:, pick_index, None, :, :], saved_sel
        )
    saved_rows = jnp.einsum(
        "gect,tex->gecx",
        order_bf,
        saved_sel.reshape(token_count, EXPERTS, -1),
        preferred_element_type=jnp.float32,
    ).astype(jnp.bfloat16)
    saved_rows = saved_rows.reshape(
        group_size, EXPERTS, part_rows, 2, group_size, hid_units
    ).transpose(0, 1, 4, 2, 3, 5)
    saved_buf = saved_rows.reshape(group_size, member_count, part_rows, 2 * hid_units)
    gate_rows = jnp.einsum("gect,te->gec", order_sel.astype(jnp.float32), gate_sel).astype(
        jnp.bfloat16
    )
    gate_buf = jnp.broadcast_to(
        gate_rows[:, :, None, :], (group_size, EXPERTS, group_size, part_rows)
    ).reshape(group_size, member_count, part_rows)
    upstream_rows = jnp.dot(
        order_bf.reshape(-1, token_count), upstream, preferred_element_type=jnp.float32
    ).astype(jnp.bfloat16)
    upstream_rows = upstream_rows.reshape(group_size, EXPERTS, 1, part_rows, model_width)
    upstream_buf = jnp.broadcast_to(
        upstream_rows, (group_size, EXPERTS, group_size, part_rows, model_width)
    )
    upstream_buf = upstream_buf.reshape(group_size, member_count, part_rows, model_width)
    recv_up, recv_saved, recv_gate = (
        lax.all_to_all(upstream_buf, "expert", split_axis=1, concat_axis=1, tiled=True),
        lax.all_to_all(saved_buf, "expert", split_axis=1, concat_axis=1, tiled=True),
        lax.all_to_all(gate_buf, "expert", split_axis=1, concat_axis=1, tiled=True),
    )
    up_flat = recv_up.reshape(-1, model_width)
    saved_flat = recv_saved.reshape(-1, 2 * hid_units)
    gate_flat = recv_gate.reshape(-1)
    gate_f = gate_flat.astype(jnp.float32)
    back_rows, down_sum = expert_rows(
        up_flat, saved_flat, gate_f, weight_gate, weight_up, weight_down
    )
    back_buf = back_rows.reshape(group_size, member_count, part_rows, model_width)
    returned = lax.all_to_all(back_buf, "expert", split_axis=1, concat_axis=1, tiled=True)
    member_sum = (
        returned.astype(jnp.float32)
        .reshape(group_size, EXPERTS, group_size, part_rows, model_width)
        .sum(axis=2)
    )
    summed = lax.optimization_barrier(member_sum.astype(jnp.bfloat16)).astype(jnp.float32)
    token_grad = lax.dot_general(
        order_sel.astype(jnp.float32).reshape(-1, token_count),
        summed.reshape(-1, model_width),
        (((0,), (0,)), ((), ())),
        precision=lax.Precision.HIGHEST,
        preferred_element_type=jnp.float32,
    )
    shifted = shifted_2(token_grad.astype(jnp.bfloat16)[None], "section", -1)
    return (shifted, down_sum.astype(jnp.bfloat16)[None])


LAST = (((1,), (1,)), ((), ()))
FIRST = (((0,), (0,)), ((), ()))
F32 = jnp.float32
BF16 = jnp.bfloat16
GATE_LANES = 128
FACTORS_COST = 8*10**8
THREE_COST = 2*10**9
K0_COST = 10 ** 10


def swapped(value, mask):
    count = lax.axis_size("expert")
    return lax.ppermute(value, "expert", [(i, i ^ mask) for i in range(count)])


def earlier_tokens(lanes):
    half = lanes // 2
    before = lax.broadcasted_iota(jnp.int32, (lanes, lanes), 0)
    after = lax.broadcasted_iota(jnp.int32, (lanes, lanes), 1)
    same = (before < half) == (after < half)
    return jnp.where(jnp.logical_and(before <= after, same), 1.0, 0.0).astype(BF16)


def earlier_kernel(out):
    out[...] = earlier_tokens(out.shape[0])


def slot_order(ids, gates, masks, cap, upto=None):
    lanes = ids.shape[1]
    half = lanes // 2
    row = lax.broadcasted_iota(jnp.int32, (8, lanes), 0)
    wanted = jnp.full((8, lanes), masks[0], jnp.int32)
    for n in range(1, len(masks)):
        wanted = jnp.where(row == n, masks[n], wanted)
    wanted = jnp.bitwise_xor(lax.axis_index("expert"), wanted)
    hit_0 = ids[0:1] == wanted
    hit_1 = ids[1:2] == wanted
    named = jnp.where(jnp.logical_or(hit_0, hit_1), 1.0, 0.0)
    gate = jnp.where(hit_0, gates[0:1], jnp.where(hit_1, gates[1:2], 0.0))
    if upto is None:
        upto = earlier_tokens(lanes)
    counts = jnp.dot(named.astype(BF16), upto, preferred_element_type=F32)
    slots = jnp.where(named > 0.5, counts.astype(jnp.int32) - 1, -1)
    slot_no = lax.broadcasted_iota(jnp.int32, (cap, lanes), 0)
    in_first = lax.broadcasted_iota(jnp.int32, (cap, lanes), 1) < half
    rows = []
    for n in range(len(masks)):
        match = jnp.where(slots[n : n + 1] == slot_no, 1.0, 0.0)
        rows.append(jnp.where(in_first, match, 0.0))
        rows.append(jnp.where(in_first, 0.0, match))
    return rows, jnp.where(hit_0, 1.0, 0.0), jnp.where(hit_1, 1.0, 0.0), gate


def gate_columns(rows, gate):
    found = [
        jnp.sum(row * gate[n // 2 : n // 2 + 1], axis=1, keepdims=True)
        for n, row in enumerate(rows)
    ]
    found = jnp.concatenate(found, axis=0)
    return jnp.broadcast_to(found, (found.shape[0], GATE_LANES)).astype(BF16)


def near_kernel(
    upto, own_ids, own_gate, own_up, own_act, pair_ids, pair_gate, pair_up, pair_act,
    up_0, near, saved_0, saved_2, saved_3, gate_0, acts,
):
    tokens = own_up.shape[0]
    cap, width = up_0.shape[0] // 2, up_0.shape[1]
    units = own_act.shape[3]
    wide = 2 * units
    ids = jnp.concatenate([own_ids[...], pair_ids[...]], axis=1)
    gates = jnp.concatenate([own_gate[...].astype(F32), pair_gate[...].astype(F32)], axis=1)
    picks = ids.shape[0]
    named = jnp.concatenate([ids.astype(F32), gates], axis=0)
    rest = jnp.zeros((2 * cap - 2 * picks, ids.shape[1]), F32)
    named = jnp.concatenate([named, rest], axis=0)
    saved_2[:, wide:] = named.astype(BF16)
    rows, hit_0, hit_1, gate = slot_order(ids, gates, (0, 2, 4, 6), cap, upto[...])
    order_bf = jnp.concatenate(rows, axis=0).astype(BF16)
    gates = gate_columns(rows[:4], gate)
    gate_0[...] = gates[: 2 * cap]
    near[:, width : width + GATE_LANES] = gates[2 * cap :]
    sel_0 = jnp.concatenate([rows[n] * hit_0[n // 2 : n // 2 + 1] for n in range(8)], axis=0)
    sel_1 = jnp.concatenate([rows[n] * hit_1[n // 2 : n // 2 + 1] for n in range(8)], axis=0)
    sel = jnp.concatenate([sel_0.astype(BF16), sel_1.astype(BF16)], axis=1)
    ups = jnp.concatenate([own_up[...], pair_up[...]], axis=0)
    picked = jnp.dot(order_bf[: 4 * cap], ups, preferred_element_type=F32)
    up_0[...] = picked[: 2 * cap].astype(BF16)
    near[:, :width] = picked[2 * cap :].astype(BF16)
    for block, act in enumerate((own_act, pair_act)):
        for pick in range(picks):
            low = (2 * pick + block) * tokens
            for side in range(2):
                part = act[:, pick, side, :]
                acts[low : low + tokens, side * units : (side + 1) * units] = part
    got = jnp.dot(sel, acts[...], preferred_element_type=F32)
    low = near.shape[1] - wide
    for n, (out, lane) in enumerate(((saved_0, 0), (near, low), (saved_2, 0), (saved_3, 0))):
        out[:, lane : lane + wide] = got[2 * cap * n : 2 * cap * (n + 1)].astype(BF16)


def read_routes(routes):
    named = routes.astype(F32)
    return named[:2].astype(jnp.int32), named[2:4]


def far_kernel(saved_2, both_up, up_2, up_3, gate_2):
    cap, width = up_2.shape[0] // 2, up_2.shape[1]
    tokens = both_up.shape[0] // 2
    ids, gates = read_routes(saved_2[:, saved_2.shape[1] - 2 * tokens :])
    rows, _, _, gate = slot_order(ids, gates, (0, 2), cap)
    order = jnp.concatenate(rows, axis=0)
    odd = lax.axis_index("expert") % 2 == 1
    order = jnp.where(odd, pltpu.roll(order, tokens, 1), order).astype(BF16)
    picked = jnp.dot(order, both_up[...], preferred_element_type=F32)
    gates = gate_columns(rows, gate)
    up_2[...] = picked[: 2 * cap].astype(BF16)
    up_3[:, :width] = picked[2 * cap :].astype(BF16)
    up_3[:, width:] = gates[2 * cap :]
    gate_2[...] = gates[: 2 * cap]


def through_expert(up, saved, gate, w_down, w_gate, w_up):
    units = w_down.shape[0]
    gate = gate[:, :1].astype(F32)
    by_a, by_b, both = factors(saved[:, :units], saved[:, units:])
    grad_h = lax.dot_general(up, w_down[...], LAST, preferred_element_type=F32) * gate
    grad_a = (grad_h * by_a).astype(BF16)
    grad_b = (grad_h * by_b).astype(BF16)
    back = lax.dot_general(grad_a, w_gate[...], LAST, preferred_element_type=F32)
    back = back + lax.dot_general(grad_b, w_up[...], LAST, preferred_element_type=F32)
    return back.astype(BF16), (gate * both).astype(BF16)


def own_kernel(up, saved, gate, beside, w_down, w_gate, w_up, back_out, scaled_out):
    width, wide = up.shape[1], saved.shape[1]
    back, scaled = through_expert(up[...], saved[...], gate[...], w_down, w_gate, w_up)
    back_out[:, :width] = back
    back_out[:, width:] = beside[:, wide:]
    scaled_out[...] = scaled


def two_kernel(up, saved, gate, w_down, w_gate, w_up, back_out, scaled_out):
    wide = 2 * w_down.shape[0]
    back, scaled = through_expert(up[...], saved[:, :wide], gate[...], w_down, w_gate, w_up)
    back_out[...] = back
    scaled_out[...] = scaled


def factors(gate_pre, up_pre):
    gate_pre, up_pre = gate_pre.astype(F32), up_pre.astype(F32)
    sig = 1.0 / (1.0 + jnp.exp(-gate_pre))
    silu = gate_pre * sig
    return up_pre * sig * (1.0 + gate_pre * (1.0 - sig)), silu, silu * up_pre


def factors_kernel(near, saved, by_a, by_b, both):
    units = by_a.shape[1]
    low = near.shape[1] - 2 * units
    gate_pre = jnp.concatenate([near[:, low : low + units], saved[:, :units]], axis=0)
    up_pre = jnp.concatenate([near[:, low + units :], saved[:, units:]], axis=0)
    by_a[...], by_b[...], both[...] = factors(gate_pre, up_pre)


def odd_kernel(
    near, up_3, by_a, by_b, both, w_down, w_gate, w_up, back_1, back_6, back_7, scaled_out
):
    each, width = back_1.shape
    gate = [near[:, width : width + 1].astype(F32), up_3[:, width : width + 1].astype(F32)]
    gate = jnp.concatenate(gate, axis=0)
    up = jnp.concatenate([near[:, :width], up_3[:, :width]], axis=0)
    grad_h = lax.dot_general(up, w_down[...], LAST, preferred_element_type=F32) * gate
    grad_a = (grad_h * by_a[...]).astype(BF16)
    grad_b = (grad_h * by_b[...]).astype(BF16)
    scaled_out[...] = (gate * both[...]).astype(BF16)
    back = lax.dot_general(grad_a, w_gate[...], LAST, preferred_element_type=F32)
    back = back + lax.dot_general(grad_b, w_up[...], LAST, preferred_element_type=F32)
    back_1[...] = back[:each].astype(BF16)
    half = each // 2
    back_6[...] = back[each : each + half].astype(BF16)
    back_7[...] = back[each + half :].astype(BF16)


def down_kernel(scaled_a, scaled_b, scaled_c, up_a, up_b, up_c, up_d, out):
    scaled = jnp.concatenate([scaled_a[...], scaled_b[...], scaled_c[...]], axis=0)
    ups = jnp.concatenate([up_a[...], up_b[...], up_c[...], up_d[...]], axis=0)
    out[...] = lax.dot_general(scaled, ups, FIRST, preferred_element_type=F32).astype(BF16)


def two_sum_kernel(rows_0, rows_2, part, order_1, order_67):
    width = part.shape[1]
    ids, gates = read_routes(rows_0[:, width:])
    order = slot_order(ids, gates, (0, 4, 2, 6, 7), rows_2.shape[0] // 2)[0]
    order_1[...] = jnp.concatenate(order[4:6], axis=0).astype(BF16)
    order_67[...] = jnp.concatenate([order[6], order[8]], axis=0).astype(BF16)
    order = jnp.concatenate(order[:4], axis=0).astype(BF16)
    rows = jnp.concatenate([rows_0[:, :width], rows_2[...]], axis=0)
    part[...] = lax.dot_general(order, rows, FIRST, preferred_element_type=F32)


def sum_kernel(order, part, rows_1, own, other):
    tokens = own.shape[0]
    back = lax.dot_general(order[...], rows_1[...], FIRST, preferred_element_type=F32)
    back = part[...] + back
    own[...] = back[:tokens]
    other[...] = back[tokens:].astype(BF16)


def three_sum_kernel(order, rows_6, rows_7, part):
    tokens = part.shape[0]
    rows = jnp.concatenate([rows_6[...].astype(F32), rows_7[...].astype(F32)], axis=0)
    back = lax.dot_general(order[...], rows.astype(BF16), FIRST, preferred_element_type=F32)
    part[...] = back[:tokens]


def last_kernel(own, other, part, out):
    out[...] = (own[...] + other[...].astype(F32) + part[...]).astype(BF16)


def local_call(kernel, outs, args, scratch=(), cost=0, limit=28, **blocks):
    whole = pl.BlockSpec(memory_space=pltpu.VMEM)
    if not blocks:
        blocks["in_specs"] = [whole] * len(args)
        blocks["out_specs"] = [whole] * len(outs)
    return pl.pallas_call(
        kernel,
        out_shape=outs,
        scratch_shapes=scratch,
        compiler_params=pltpu.CompilerParams(vmem_limit_bytes=limit * 1024 * 1024),
        cost_estimate=pl.CostEstimate(flops=cost, bytes_accessed=0, transcendentals=0),
        **blocks,
    )(*args)


def after(value, *others):
    return lax.optimization_barrier((value,) + others)[0]


def before_section(value, mask):
    sections, count = lax.axis_size("section"), lax.axis_size("expert")
    pairs = [
        (s * count + e, (s + sections - 1) % sections * count + (e ^ mask))
        for s in range(sections)
        for e in range(count)
    ]
    return lax.ppermute(value, ("section", "expert"), pairs)


def on_device_pairs(grad_out, pre_act, route_ids, route_gate, w_gate, w_up, w_down):
    tokens, width = grad_out.shape[1:]
    units = w_down.shape[1]
    wide = 2 * units
    cap = 3 * tokens // 8
    upstream = grad_out[0]

    def shape(rows, lanes):
        return jax.ShapeDtypeStruct((rows, lanes), BF16)

    up, act = grad_out[0], pre_act[0]
    ids, gate = route_ids[0].T, route_gate[0].T
    far_up = swapped(up, 4)
    (upto,) = local_call(earlier_kernel, [shape(2 * tokens, 2 * tokens)], (), cost=K0_COST)
    own_rows, near_rows, saved_0, saved_2, saved_3, gate_0 = local_call(
        near_kernel,
        [shape(2 * cap, width), shape(2 * cap, width + GATE_LANES + wide)]
        + [shape(2 * cap, wide), shape(2 * cap, wide + 2 * tokens), shape(2 * cap, wide)]
        + [shape(2 * cap, GATE_LANES)],
        (upto, ids, gate, up, act, swapped(ids, 1), swapped(gate, 1), swapped(up, 1), swapped(act, 1)),
        [pltpu.VMEM((4 * tokens, wide), BF16)],
    )
    near_rows = swapped(near_rows, 2)
    beside, saved_2 = saved_2, swapped(saved_2, 4)
    weights = (w_down[0], w_gate[0], w_up[0])
    back_0, scaled_0 = local_call(
        own_kernel,
        [shape(2 * cap, width + 2 * tokens), shape(2 * cap, units)],
        (own_rows, saved_0, gate_0, beside, *weights),
    )
    far_up = after(far_up, back_0)
    far_both = lax.all_gather(
        far_up, "expert", axis=0, tiled=True, axis_index_groups=[[i, i + 1] for i in range(0, 8, 2)]
    )
    saved_3 = swapped(after(saved_3, far_both), 6)
    two_rows, three_rows, gate_2 = local_call(
        far_kernel,
        [shape(2 * cap, width), shape(2 * cap, width + GATE_LANES), shape(2 * cap, GATE_LANES)],
        (saved_2, far_both),
    )
    three_rows = swapped(three_rows, 2)
    home_0 = before_section(back_0, 0)
    two_rows = after(two_rows, home_0)
    back_2, scaled_2 = local_call(
        two_kernel,
        [shape(2 * cap, width), shape(2 * cap, units)],
        (two_rows, saved_2, gate_2, *weights),
    )
    saved_3 = after(saved_3, back_2)
    by_saved = local_call(
        factors_kernel,
        [jax.ShapeDtypeStruct((4 * cap, units), F32)] * 3,
        (near_rows, saved_3),
        cost=FACTORS_COST,
    )
    back_1, back_6, back_7, scaled_13 = local_call(
        odd_kernel,
        [shape(2 * cap, width)] + [shape(cap, width)] * 2 + [shape(4 * cap, units)],
        (near_rows, three_rows, *by_saved, *weights),
    )
    home_2 = before_section(back_2, 4)
    home_1 = before_section(back_1, 2)
    rows_6 = before_section(back_6, 6)
    rows_7 = before_section(back_7, 7)
    parts = 4

    def columns(array):
        return pl.BlockSpec((array.shape[0], width // parts), lambda n: (0, n))

    def every(array):
        return pl.BlockSpec(array.shape, lambda n: (0, 0))

    scaled = (scaled_0, scaled_2, scaled_13)
    ups = (own_rows, two_rows, near_rows, three_rows)
    (down,) = local_call(
        down_kernel,
        [shape(units, width)],
        scaled + ups,
        grid=(parts,),
        in_specs=[every(a) for a in scaled] + [columns(a) for a in ups],
        out_specs=[pl.BlockSpec((units, width // parts), lambda n: (0, n))],
    )
    home_2 = after(home_2, down)
    part, order_1, order_67 = local_call(
        two_sum_kernel,
        [jax.ShapeDtypeStruct((2 * tokens, width), F32)]
        + [shape(2 * cap, 2 * tokens)] * 2,
        (home_0, home_2),
    )
    rows_6 = after(rows_6, part)
    summed, other = local_call(
        sum_kernel,
        [jax.ShapeDtypeStruct((tokens, width), F32), shape(tokens, width)],
        (order_1, part, home_1),
    )
    other = swapped(other, 1)
    (three,) = local_call(
        three_sum_kernel,
        [jax.ShapeDtypeStruct((tokens, width), F32)],
        (order_67, rows_6, rows_7),
        cost=THREE_COST,
    )
    (total,) = local_call(last_kernel, [shape(tokens, width)], (summed, other, three))
    return total[None], down[None]


def on_device(*args):
    if lax.axis_size("expert") == EXPERTS:
        return on_device_pairs(*args)
    return on_device_general(*args)


def solution(mesh):
    placed = (
        P("section", "expert", None),
        P("section", "expert", None, None, None),
        P("section", "expert", None),
        P("section", "expert", None),
        P("section", None, "expert"),
        P("section", None, "expert"),
        P("section", "expert", None),
    )
    return jax.shard_map(
        on_device,
        mesh=mesh,
        in_specs=placed,
        out_specs=(P("section", "expert", None), P("section", "expert", None)),
        check_vma=False,
    )
```

```python
import jax
import jax.numpy as jnp
from jax import lax
from jax.experimental import pallas as pl
from jax.experimental.pallas import tpu as pltpu
from jax.sharding import PartitionSpec as P

EXPERTS = 8


def shifted_2(value, axis, steps):
    count = lax.axis_size(axis)
    pairs = [(source, (source + steps) % count) for source in range(count)]
    return lax.ppermute(value, axis, pairs)


def expert_rows(upstream, saved_rows, gate_rows, weight_gate, weight_up, weight_down):
    hid_units = weight_down.shape[0]
    grad_hidden = (
        lax.dot_general(
            upstream, weight_down, (((1,), (1,)), ((), ())), preferred_element_type=jnp.float32
        )
        * gate_rows[:, None]
    )
    saved_f = saved_rows.astype(jnp.float32)
    gate_pre = saved_f[:, :hid_units]
    up_pre = saved_f[:, hid_units:]
    sigmoid_g = jax.nn.sigmoid(gate_pre)
    silu_val = gate_pre * sigmoid_g
    grad_gate = (grad_hidden * up_pre * sigmoid_g * (1.0 + gate_pre * (1.0 - sigmoid_g))).astype(
        jnp.bfloat16
    )
    grad_upper = (grad_hidden * silu_val).astype(jnp.bfloat16)
    scaled_hidden = (gate_rows[:, None] * silu_val * up_pre).astype(jnp.bfloat16)
    contract_last = (((1,), (1,)), ((), ()))
    back_rows = lax.dot_general(
        grad_gate, weight_gate, contract_last, preferred_element_type=jnp.float32
    )
    back_rows = (
        back_rows
        + lax.dot_general(grad_upper, weight_up, contract_last, preferred_element_type=jnp.float32)
    ).astype(jnp.bfloat16)
    weight_term = lax.dot_general(
        scaled_hidden, upstream, (((0,), (0,)), ((), ())), preferred_element_type=jnp.float32
    )
    return (back_rows, weight_term)


def on_device_general(grad_out, pre_act, route_ids, route_gate, w_gate, w_up, w_down):
    member_count = lax.axis_size("expert")
    group_size = member_count // EXPERTS
    token_count = grad_out.shape[1]
    model_width = grad_out.shape[2]
    hid_units = w_down.shape[1]
    slot_cap = 3 * token_count // 8
    part_rows = slot_cap // group_size
    upstream = grad_out[0]
    route_rows = route_ids[0]
    gate_vals = route_gate[0]
    saved_acts = pre_act[0]
    weight_gate = w_gate[0]
    weight_up = w_up[0]
    weight_down = w_down[0]
    picked = route_rows[:, :, None] == jnp.arange(EXPERTS, dtype=jnp.int32)[None, None, :]
    is_named = jnp.any(picked, axis=1).astype(jnp.int32)
    slot_rank = jnp.cumsum(is_named, axis=0) - 1
    slot_index = jnp.where(is_named > 0, slot_rank, -1)
    selector = slot_index.T[:, None, :] == jnp.arange(slot_cap, dtype=jnp.int32)[None, :, None]
    order_sel = selector.reshape(EXPERTS, group_size, part_rows, token_count).transpose(1, 0, 2, 3)
    order_bf = order_sel.astype(jnp.bfloat16)
    gate_sel = jnp.sum(jnp.where(picked, gate_vals[:, :, None].astype(jnp.float32), 0.0), axis=1)
    saved_sel = jnp.zeros((token_count, EXPERTS, 2, saved_acts.shape[3]), jnp.bfloat16)
    for pick_index in range(saved_acts.shape[1]):
        saved_sel = jnp.where(
            picked[:, pick_index, :, None, None], saved_acts[:, pick_index, None, :, :], saved_sel
        )
    saved_rows = jnp.einsum(
        "gect,tex->gecx",
        order_bf,
        saved_sel.reshape(token_count, EXPERTS, -1),
        preferred_element_type=jnp.float32,
    ).astype(jnp.bfloat16)
    saved_rows = saved_rows.reshape(
        group_size, EXPERTS, part_rows, 2, group_size, hid_units
    ).transpose(0, 1, 4, 2, 3, 5)
    saved_buf = saved_rows.reshape(group_size, member_count, part_rows, 2 * hid_units)
    gate_rows = jnp.einsum("gect,te->gec", order_sel.astype(jnp.float32), gate_sel).astype(
        jnp.bfloat16
    )
    gate_buf = jnp.broadcast_to(
        gate_rows[:, :, None, :], (group_size, EXPERTS, group_size, part_rows)
    ).reshape(group_size, member_count, part_rows)
    upstream_rows = jnp.dot(
        order_bf.reshape(-1, token_count), upstream, preferred_element_type=jnp.float32
    ).astype(jnp.bfloat16)
    upstream_rows = upstream_rows.reshape(group_size, EXPERTS, 1, part_rows, model_width)
    upstream_buf = jnp.broadcast_to(
        upstream_rows, (group_size, EXPERTS, group_size, part_rows, model_width)
    )
    upstream_buf = upstream_buf.reshape(group_size, member_count, part_rows, model_width)
    recv_up, recv_saved, recv_gate = (
        lax.all_to_all(upstream_buf, "expert", split_axis=1, concat_axis=1, tiled=True),
        lax.all_to_all(saved_buf, "expert", split_axis=1, concat_axis=1, tiled=True),
        lax.all_to_all(gate_buf, "expert", split_axis=1, concat_axis=1, tiled=True),
    )
    up_flat = recv_up.reshape(-1, model_width)
    saved_flat = recv_saved.reshape(-1, 2 * hid_units)
    gate_flat = recv_gate.reshape(-1)
    gate_f = gate_flat.astype(jnp.float32)
    back_rows, down_sum = expert_rows(
        up_flat, saved_flat, gate_f, weight_gate, weight_up, weight_down
    )
    back_buf = back_rows.reshape(group_size, member_count, part_rows, model_width)
    returned = lax.all_to_all(back_buf, "expert", split_axis=1, concat_axis=1, tiled=True)
    member_sum = (
        returned.astype(jnp.float32)
        .reshape(group_size, EXPERTS, group_size, part_rows, model_width)
        .sum(axis=2)
    )
    summed = lax.optimization_barrier(member_sum.astype(jnp.bfloat16)).astype(jnp.float32)
    token_grad = lax.dot_general(
        order_sel.astype(jnp.float32).reshape(-1, token_count),
        summed.reshape(-1, model_width),
        (((0,), (0,)), ((), ())),
        precision=lax.Precision.HIGHEST,
        preferred_element_type=jnp.float32,
    )
    shifted = shifted_2(token_grad.astype(jnp.bfloat16)[None], "section", -1)
    return (shifted, down_sum.astype(jnp.bfloat16)[None])


LAST = (((1,), (1,)), ((), ()))
FIRST = (((0,), (0,)), ((), ()))
F32 = jnp.float32
BF16 = jnp.bfloat16
GATE_LANES = 128
FACTORS_COST = 8*10**8
THREE_COST = 2*10**9
K0_COST = 10 ** 10


def swapped(value, mask):
    count = lax.axis_size("expert")
    return lax.ppermute(value, "expert", [(i, i ^ mask) for i in range(count)])


def earlier_tokens(lanes):
    half = lanes // 2
    before = lax.broadcasted_iota(jnp.int32, (lanes, lanes), 0)
    after = lax.broadcasted_iota(jnp.int32, (lanes, lanes), 1)
    same = (before < half) == (after < half)
    return jnp.where(jnp.logical_and(before <= after, same), 1.0, 0.0).astype(BF16)


def earlier_kernel(out):
    out[...] = earlier_tokens(out.shape[0])


def slot_order(ids, gates, masks, cap, upto=None):
    lanes = ids.shape[1]
    half = lanes // 2
    row = lax.broadcasted_iota(jnp.int32, (8, lanes), 0)
    wanted = jnp.full((8, lanes), masks[0], jnp.int32)
    for n in range(1, len(masks)):
        wanted = jnp.where(row == n, masks[n], wanted)
    wanted = jnp.bitwise_xor(lax.axis_index("expert"), wanted)
    hit_0 = ids[0:1] == wanted
    hit_1 = ids[1:2] == wanted
    named = jnp.where(jnp.logical_or(hit_0, hit_1), 1.0, 0.0)
    gate = jnp.where(hit_0, gates[0:1], jnp.where(hit_1, gates[1:2], 0.0))
    if upto is None:
        upto = earlier_tokens(lanes)
    counts = jnp.dot(named.astype(BF16), upto, preferred_element_type=F32)
    slots = jnp.where(named > 0.5, counts.astype(jnp.int32) - 1, -1)
    slot_no = lax.broadcasted_iota(jnp.int32, (cap, lanes), 0)
    in_first = lax.broadcasted_iota(jnp.int32, (cap, lanes), 1) < half
    rows = []
    for n in range(len(masks)):
        match = jnp.where(slots[n : n + 1] == slot_no, 1.0, 0.0)
        rows.append(jnp.where(in_first, match, 0.0))
        rows.append(jnp.where(in_first, 0.0, match))
    return rows, jnp.where(hit_0, 1.0, 0.0), jnp.where(hit_1, 1.0, 0.0), gate


def gate_columns(rows, gate):
    found = [
        jnp.sum(row * gate[n // 2 : n // 2 + 1], axis=1, keepdims=True)
        for n, row in enumerate(rows)
    ]
    found = jnp.concatenate(found, axis=0)
    return jnp.broadcast_to(found, (found.shape[0], GATE_LANES)).astype(BF16)


def near_kernel(
    upto, own_ids, own_gate, own_up, own_act, pair_ids, pair_gate, pair_up, pair_act,
    up_0, near, saved_0, saved_2, saved_3, gate_0, acts,
):
    tokens = own_up.shape[0]
    cap, width = up_0.shape[0] // 2, up_0.shape[1]
    units = own_act.shape[3]
    wide = 2 * units
    ids = jnp.concatenate([own_ids[...], pair_ids[...]], axis=1)
    gates = jnp.concatenate([own_gate[...].astype(F32), pair_gate[...].astype(F32)], axis=1)
    picks = ids.shape[0]
    named = jnp.concatenate([ids.astype(F32), gates], axis=0)
    rest = jnp.zeros((2 * cap - 2 * picks, ids.shape[1]), F32)
    named = jnp.concatenate([named, rest], axis=0)
    saved_2[:, wide:] = named.astype(BF16)
    rows, hit_0, hit_1, gate = slot_order(ids, gates, (0, 2, 4, 6), cap, upto[...])
    order_bf = jnp.concatenate(rows, axis=0).astype(BF16)
    gates = gate_columns(rows[:4], gate)
    gate_0[...] = gates[: 2 * cap]
    near[:, width : width + GATE_LANES] = gates[2 * cap :]
    sel_0 = jnp.concatenate([rows[n] * hit_0[n // 2 : n // 2 + 1] for n in range(8)], axis=0)
    sel_1 = jnp.concatenate([rows[n] * hit_1[n // 2 : n // 2 + 1] for n in range(8)], axis=0)
    sel = jnp.concatenate([sel_0.astype(BF16), sel_1.astype(BF16)], axis=1)
    ups = jnp.concatenate([own_up[...], pair_up[...]], axis=0)
    picked = jnp.dot(order_bf[: 4 * cap], ups, preferred_element_type=F32)
    up_0[...] = picked[: 2 * cap].astype(BF16)
    near[:, :width] = picked[2 * cap :].astype(BF16)
    for block, act in enumerate((own_act, pair_act)):
        for pick in range(picks):
            low = (2 * pick + block) * tokens
            for side in range(2):
                part = act[:, pick, side, :]
                acts[low : low + tokens, side * units : (side + 1) * units] = part
    got = jnp.dot(sel, acts[...], preferred_element_type=F32)
    low = near.shape[1] - wide
    for n, (out, lane) in enumerate(((saved_0, 0), (near, low), (saved_2, 0), (saved_3, 0))):
        out[:, lane : lane + wide] = got[2 * cap * n : 2 * cap * (n + 1)].astype(BF16)


def read_routes(routes):
    named = routes.astype(F32)
    return named[:2].astype(jnp.int32), named[2:4]


def far_kernel(saved_2, both_up, up_2, up_3, gate_2):
    cap, width = up_2.shape[0] // 2, up_2.shape[1]
    tokens = both_up.shape[0] // 2
    ids, gates = read_routes(saved_2[:, saved_2.shape[1] - 2 * tokens :])
    rows, _, _, gate = slot_order(ids, gates, (0, 2), cap)
    order = jnp.concatenate(rows, axis=0)
    odd = lax.axis_index("expert") % 2 == 1
    order = jnp.where(odd, pltpu.roll(order, tokens, 1), order).astype(BF16)
    picked = jnp.dot(order, both_up[...], preferred_element_type=F32)
    gates = gate_columns(rows, gate)
    up_2[...] = picked[: 2 * cap].astype(BF16)
    up_3[:, :width] = picked[2 * cap :].astype(BF16)
    up_3[:, width:] = gates[2 * cap :]
    gate_2[...] = gates[: 2 * cap]


def through_expert(up, saved, gate, w_down, w_gate, w_up):
    units = w_down.shape[0]
    gate = gate[:, :1].astype(F32)
    by_a, by_b, both = factors(saved[:, :units], saved[:, units:])
    grad_h = lax.dot_general(up, w_down[...], LAST, preferred_element_type=F32) * gate
    grad_a = (grad_h * by_a).astype(BF16)
    grad_b = (grad_h * by_b).astype(BF16)
    back = lax.dot_general(grad_a, w_gate[...], LAST, preferred_element_type=F32)
    back = back + lax.dot_general(grad_b, w_up[...], LAST, preferred_element_type=F32)
    return back.astype(BF16), (gate * both).astype(BF16)


def own_kernel(up, saved, gate, beside, w_down, w_gate, w_up, back_out, scaled_out):
    width, wide = up.shape[1], saved.shape[1]
    back, scaled = through_expert(up[...], saved[...], gate[...], w_down, w_gate, w_up)
    back_out[:, :width] = back
    back_out[:, width:] = beside[:, wide:]
    scaled_out[...] = scaled


def two_kernel(up, saved, gate, w_down, w_gate, w_up, back_out, scaled_out):
    wide = 2 * w_down.shape[0]
    back, scaled = through_expert(up[...], saved[:, :wide], gate[...], w_down, w_gate, w_up)
    back_out[...] = back
    scaled_out[...] = scaled


def factors(gate_pre, up_pre):
    gate_pre, up_pre = gate_pre.astype(F32), up_pre.astype(F32)
    sig = 1.0 / (1.0 + jnp.exp(-gate_pre))
    silu = gate_pre * sig
    return up_pre * sig * (1.0 + gate_pre * (1.0 - sig)), silu, silu * up_pre


def factors_kernel(near, saved, by_a, by_b, both):
    units = by_a.shape[1]
    low = near.shape[1] - 2 * units
    gate_pre = jnp.concatenate([near[:, low : low + units], saved[:, :units]], axis=0)
    up_pre = jnp.concatenate([near[:, low + units :], saved[:, units:]], axis=0)
    by_a[...], by_b[...], both[...] = factors(gate_pre, up_pre)


def odd_kernel(
    near, up_3, by_a, by_b, both, w_down, w_gate, w_up, back_1, back_6, back_7, scaled_out
):
    each, width = back_1.shape
    gate = [near[:, width : width + 1].astype(F32), up_3[:, width : width + 1].astype(F32)]
    gate = jnp.concatenate(gate, axis=0)
    up = jnp.concatenate([near[:, :width], up_3[:, :width]], axis=0)
    grad_h = lax.dot_general(up, w_down[...], LAST, preferred_element_type=F32) * gate
    grad_a = (grad_h * by_a[...]).astype(BF16)
    grad_b = (grad_h * by_b[...]).astype(BF16)
    scaled_out[...] = (gate * both[...]).astype(BF16)
    back = lax.dot_general(grad_a, w_gate[...], LAST, preferred_element_type=F32)
    back = back + lax.dot_general(grad_b, w_up[...], LAST, preferred_element_type=F32)
    back_1[...] = back[:each].astype(BF16)
    half = each // 2
    back_6[...] = back[each : each + half].astype(BF16)
    back_7[...] = back[each + half :].astype(BF16)


def down_kernel(scaled_a, scaled_b, scaled_c, up_a, up_b, up_c, up_d, out):
    scaled = jnp.concatenate([scaled_a[...], scaled_b[...], scaled_c[...]], axis=0)
    ups = jnp.concatenate([up_a[...], up_b[...], up_c[...], up_d[...]], axis=0)
    out[...] = lax.dot_general(scaled, ups, FIRST, preferred_element_type=F32).astype(BF16)


def two_sum_kernel(rows_0, rows_2, part, order_1, order_67):
    width = part.shape[1]
    ids, gates = read_routes(rows_0[:, width:])
    order = slot_order(ids, gates, (0, 4, 2, 6, 7), rows_2.shape[0] // 2)[0]
    order_1[...] = jnp.concatenate(order[4:6], axis=0).astype(BF16)
    order_67[...] = jnp.concatenate([order[6], order[8]], axis=0).astype(BF16)
    order = jnp.concatenate(order[:4], axis=0).astype(BF16)
    rows = jnp.concatenate([rows_0[:, :width], rows_2[...]], axis=0)
    part[...] = lax.dot_general(order, rows, FIRST, preferred_element_type=F32)


def sum_kernel(order, part, rows_1, own, other):
    tokens = own.shape[0]
    back = lax.dot_general(order[...], rows_1[...], FIRST, preferred_element_type=F32)
    back = part[...] + back
    own[...] = back[:tokens]
    other[...] = back[tokens:].astype(BF16)


def three_sum_kernel(order, rows_6, rows_7, part):
    tokens = part.shape[0]
    rows = jnp.concatenate([rows_6[...].astype(F32), rows_7[...].astype(F32)], axis=0)
    back = lax.dot_general(order[...], rows.astype(BF16), FIRST, preferred_element_type=F32)
    part[...] = back[:tokens]


def last_kernel(own, other, part, out, done, sent):
    pieces = 4
    each = own.shape[1] // pieces
    copies = []
    for n in range(pieces):
        lanes = pl.ds(n * each, each)
        total = own[:, lanes] + other[:, lanes].astype(F32) + part[:, lanes]
        done[:, lanes] = total.astype(BF16)
        copies.append(pltpu.make_async_copy(done.at[:, lanes], out.at[:, lanes], sent.at[n]))
        copies[-1].start()
    for copy in copies:
        copy.wait()


def local_call(kernel, outs, args, scratch=(), cost=0, limit=28, **blocks):
    whole = pl.BlockSpec(memory_space=pltpu.VMEM)
    if not blocks:
        blocks["in_specs"] = [whole] * len(args)
        blocks["out_specs"] = [whole] * len(outs)
    return pl.pallas_call(
        kernel,
        out_shape=outs,
        scratch_shapes=scratch,
        compiler_params=pltpu.CompilerParams(vmem_limit_bytes=limit * 1024 * 1024),
        cost_estimate=pl.CostEstimate(flops=cost, bytes_accessed=0, transcendentals=0),
        **blocks,
    )(*args)


def after(value, *others):
    return lax.optimization_barrier((value,) + others)[0]


def before_section(value, mask):
    sections, count = lax.axis_size("section"), lax.axis_size("expert")
    pairs = [
        (s * count + e, (s + sections - 1) % sections * count + (e ^ mask))
        for s in range(sections)
        for e in range(count)
    ]
    return lax.ppermute(value, ("section", "expert"), pairs)


def on_device_pairs(grad_out, pre_act, route_ids, route_gate, w_gate, w_up, w_down):
    tokens, width = grad_out.shape[1:]
    units = w_down.shape[1]
    wide = 2 * units
    cap = 3 * tokens // 8
    upstream = grad_out[0]

    def shape(rows, lanes):
        return jax.ShapeDtypeStruct((rows, lanes), BF16)

    up, act = grad_out[0], pre_act[0]
    ids, gate = route_ids[0].T, route_gate[0].T
    far_up = swapped(up, 4)
    (upto,) = local_call(earlier_kernel, [shape(2 * tokens, 2 * tokens)], (), cost=K0_COST)
    own_rows, near_rows, saved_0, saved_2, saved_3, gate_0 = local_call(
        near_kernel,
        [shape(2 * cap, width), shape(2 * cap, width + GATE_LANES + wide)]
        + [shape(2 * cap, wide), shape(2 * cap, wide + 2 * tokens), shape(2 * cap, wide)]
        + [shape(2 * cap, GATE_LANES)],
        (upto, ids, gate, up, act, swapped(ids, 1), swapped(gate, 1), swapped(up, 1), swapped(act, 1)),
        [pltpu.VMEM((4 * tokens, wide), BF16)],
    )
    near_rows = swapped(near_rows, 2)
    beside, saved_2 = saved_2, swapped(saved_2, 4)
    weights = (w_down[0], w_gate[0], w_up[0])
    back_0, scaled_0 = local_call(
        own_kernel,
        [shape(2 * cap, width + 2 * tokens), shape(2 * cap, units)],
        (own_rows, saved_0, gate_0, beside, *weights),
    )
    far_up = after(far_up, back_0)
    far_both = lax.all_gather(
        far_up, "expert", axis=0, tiled=True, axis_index_groups=[[i, i + 1] for i in range(0, 8, 2)]
    )
    saved_3 = swapped(after(saved_3, far_both), 6)
    two_rows, three_rows, gate_2 = local_call(
        far_kernel,
        [shape(2 * cap, width), shape(2 * cap, width + GATE_LANES), shape(2 * cap, GATE_LANES)],
        (saved_2, far_both),
    )
    three_rows = swapped(three_rows, 2)
    home_0 = before_section(back_0, 0)
    two_rows = after(two_rows, home_0)
    back_2, scaled_2 = local_call(
        two_kernel,
        [shape(2 * cap, width), shape(2 * cap, units)],
        (two_rows, saved_2, gate_2, *weights),
    )
    saved_3 = after(saved_3, back_2)
    by_saved = local_call(
        factors_kernel,
        [jax.ShapeDtypeStruct((4 * cap, units), F32)] * 3,
        (near_rows, saved_3),
        cost=FACTORS_COST,
    )
    back_1, back_6, back_7, scaled_13 = local_call(
        odd_kernel,
        [shape(2 * cap, width)] + [shape(cap, width)] * 2 + [shape(4 * cap, units)],
        (near_rows, three_rows, *by_saved, *weights),
    )
    home_2 = before_section(back_2, 4)
    home_1 = before_section(back_1, 2)
    rows_6 = before_section(back_6, 6)
    rows_7 = before_section(back_7, 7)
    parts = 4

    def columns(array):
        return pl.BlockSpec((array.shape[0], width // parts), lambda n: (0, n))

    def every(array):
        return pl.BlockSpec(array.shape, lambda n: (0, 0))

    scaled = (scaled_0, scaled_2, scaled_13)
    ups = (own_rows, two_rows, near_rows, three_rows)
    (down,) = local_call(
        down_kernel,
        [shape(units, width)],
        scaled + ups,
        grid=(parts,),
        in_specs=[every(a) for a in scaled] + [columns(a) for a in ups],
        out_specs=[pl.BlockSpec((units, width // parts), lambda n: (0, n))],
    )
    home_2 = after(home_2, down)
    part, order_1, order_67 = local_call(
        two_sum_kernel,
        [jax.ShapeDtypeStruct((2 * tokens, width), F32)]
        + [shape(2 * cap, 2 * tokens)] * 2,
        (home_0, home_2),
    )
    rows_6 = after(rows_6, part)
    summed, other = local_call(
        sum_kernel,
        [jax.ShapeDtypeStruct((tokens, width), F32), shape(tokens, width)],
        (order_1, part, home_1),
    )
    other = swapped(other, 1)
    (three,) = local_call(
        three_sum_kernel,
        [jax.ShapeDtypeStruct((tokens, width), F32)],
        (order_67, rows_6, rows_7),
        cost=THREE_COST,
    )
    vmem = pl.BlockSpec(memory_space=pltpu.VMEM)
    (total,) = local_call(
        last_kernel,
        [shape(tokens, width)],
        (summed, other, three),
        [pltpu.VMEM((tokens, width), BF16), pltpu.SemaphoreType.DMA((4,))],
        in_specs=[vmem] * 3,
        out_specs=[pl.BlockSpec(memory_space=pltpu.HBM)],
    )
    return total[None], down[None]


def on_device(*args):
    if lax.axis_size("expert") == EXPERTS:
        return on_device_pairs(*args)
    return on_device_general(*args)


def solution(mesh):
    placed = (
        P("section", "expert", None),
        P("section", "expert", None, None, None),
        P("section", "expert", None),
        P("section", "expert", None),
        P("section", None, "expert"),
        P("section", None, "expert"),
        P("section", "expert", None),
    )
    return jax.shard_map(
        on_device,
        mesh=mesh,
        in_specs=placed,
        out_specs=(P("section", "expert", None), P("section", "expert", None)),
        check_vma=False,
    )
```

```python
import jax
import jax.numpy as jnp
from jax import lax
from jax.experimental import pallas as pl
from jax.experimental.pallas import tpu as pltpu
from jax.sharding import PartitionSpec as P

EXPERTS = 8


def shifted_2(value, axis, steps):
    count = lax.axis_size(axis)
    pairs = [(source, (source + steps) % count) for source in range(count)]
    return lax.ppermute(value, axis, pairs)


def expert_rows(upstream, saved_rows, gate_rows, weight_gate, weight_up, weight_down):
    hid_units = weight_down.shape[0]
    grad_hidden = (
        lax.dot_general(
            upstream, weight_down, (((1,), (1,)), ((), ())), preferred_element_type=jnp.float32
        )
        * gate_rows[:, None]
    )
    saved_f = saved_rows.astype(jnp.float32)
    gate_pre = saved_f[:, :hid_units]
    up_pre = saved_f[:, hid_units:]
    sigmoid_g = jax.nn.sigmoid(gate_pre)
    silu_val = gate_pre * sigmoid_g
    grad_gate = (grad_hidden * up_pre * sigmoid_g * (1.0 + gate_pre * (1.0 - sigmoid_g))).astype(
        jnp.bfloat16
    )
    grad_upper = (grad_hidden * silu_val).astype(jnp.bfloat16)
    scaled_hidden = (gate_rows[:, None] * silu_val * up_pre).astype(jnp.bfloat16)
    contract_last = (((1,), (1,)), ((), ()))
    back_rows = lax.dot_general(
        grad_gate, weight_gate, contract_last, preferred_element_type=jnp.float32
    )
    back_rows = (
        back_rows
        + lax.dot_general(grad_upper, weight_up, contract_last, preferred_element_type=jnp.float32)
    ).astype(jnp.bfloat16)
    weight_term = lax.dot_general(
        scaled_hidden, upstream, (((0,), (0,)), ((), ())), preferred_element_type=jnp.float32
    )
    return (back_rows, weight_term)


def on_device_general(grad_out, pre_act, route_ids, route_gate, w_gate, w_up, w_down):
    member_count = lax.axis_size("expert")
    group_size = member_count // EXPERTS
    token_count = grad_out.shape[1]
    model_width = grad_out.shape[2]
    hid_units = w_down.shape[1]
    slot_cap = 3 * token_count // 8
    part_rows = slot_cap // group_size
    upstream = grad_out[0]
    route_rows = route_ids[0]
    gate_vals = route_gate[0]
    saved_acts = pre_act[0]
    weight_gate = w_gate[0]
    weight_up = w_up[0]
    weight_down = w_down[0]
    picked = route_rows[:, :, None] == jnp.arange(EXPERTS, dtype=jnp.int32)[None, None, :]
    is_named = jnp.any(picked, axis=1).astype(jnp.int32)
    slot_rank = jnp.cumsum(is_named, axis=0) - 1
    slot_index = jnp.where(is_named > 0, slot_rank, -1)
    selector = slot_index.T[:, None, :] == jnp.arange(slot_cap, dtype=jnp.int32)[None, :, None]
    order_sel = selector.reshape(EXPERTS, group_size, part_rows, token_count).transpose(1, 0, 2, 3)
    order_bf = order_sel.astype(jnp.bfloat16)
    gate_sel = jnp.sum(jnp.where(picked, gate_vals[:, :, None].astype(jnp.float32), 0.0), axis=1)
    saved_sel = jnp.zeros((token_count, EXPERTS, 2, saved_acts.shape[3]), jnp.bfloat16)
    for pick_index in range(saved_acts.shape[1]):
        saved_sel = jnp.where(
            picked[:, pick_index, :, None, None], saved_acts[:, pick_index, None, :, :], saved_sel
        )
    saved_rows = jnp.einsum(
        "gect,tex->gecx",
        order_bf,
        saved_sel.reshape(token_count, EXPERTS, -1),
        preferred_element_type=jnp.float32,
    ).astype(jnp.bfloat16)
    saved_rows = saved_rows.reshape(
        group_size, EXPERTS, part_rows, 2, group_size, hid_units
    ).transpose(0, 1, 4, 2, 3, 5)
    saved_buf = saved_rows.reshape(group_size, member_count, part_rows, 2 * hid_units)
    gate_rows = jnp.einsum("gect,te->gec", order_sel.astype(jnp.float32), gate_sel).astype(
        jnp.bfloat16
    )
    gate_buf = jnp.broadcast_to(
        gate_rows[:, :, None, :], (group_size, EXPERTS, group_size, part_rows)
    ).reshape(group_size, member_count, part_rows)
    upstream_rows = jnp.dot(
        order_bf.reshape(-1, token_count), upstream, preferred_element_type=jnp.float32
    ).astype(jnp.bfloat16)
    upstream_rows = upstream_rows.reshape(group_size, EXPERTS, 1, part_rows, model_width)
    upstream_buf = jnp.broadcast_to(
        upstream_rows, (group_size, EXPERTS, group_size, part_rows, model_width)
    )
    upstream_buf = upstream_buf.reshape(group_size, member_count, part_rows, model_width)
    recv_up, recv_saved, recv_gate = (
        lax.all_to_all(upstream_buf, "expert", split_axis=1, concat_axis=1, tiled=True),
        lax.all_to_all(saved_buf, "expert", split_axis=1, concat_axis=1, tiled=True),
        lax.all_to_all(gate_buf, "expert", split_axis=1, concat_axis=1, tiled=True),
    )
    up_flat = recv_up.reshape(-1, model_width)
    saved_flat = recv_saved.reshape(-1, 2 * hid_units)
    gate_flat = recv_gate.reshape(-1)
    gate_f = gate_flat.astype(jnp.float32)
    back_rows, down_sum = expert_rows(
        up_flat, saved_flat, gate_f, weight_gate, weight_up, weight_down
    )
    back_buf = back_rows.reshape(group_size, member_count, part_rows, model_width)
    returned = lax.all_to_all(back_buf, "expert", split_axis=1, concat_axis=1, tiled=True)
    member_sum = (
        returned.astype(jnp.float32)
        .reshape(group_size, EXPERTS, group_size, part_rows, model_width)
        .sum(axis=2)
    )
    summed = lax.optimization_barrier(member_sum.astype(jnp.bfloat16)).astype(jnp.float32)
    token_grad = lax.dot_general(
        order_sel.astype(jnp.float32).reshape(-1, token_count),
        summed.reshape(-1, model_width),
        (((0,), (0,)), ((), ())),
        precision=lax.Precision.HIGHEST,
        preferred_element_type=jnp.float32,
    )
    shifted = shifted_2(token_grad.astype(jnp.bfloat16)[None], "section", -1)
    return (shifted, down_sum.astype(jnp.bfloat16)[None])


LAST = (((1,), (1,)), ((), ()))
FIRST = (((0,), (0,)), ((), ()))
F32 = jnp.float32
BF16 = jnp.bfloat16
GATE_LANES = 128
FACTORS_COST = 8*10**8
THREE_COST = 5 * 10**9
K0_COST = 10 ** 10


def swapped(value, mask):
    count = lax.axis_size("expert")
    return lax.ppermute(value, "expert", [(i, i ^ mask) for i in range(count)])


def earlier_tokens(lanes):
    half = lanes // 2
    before = lax.broadcasted_iota(jnp.int32, (lanes, lanes), 0)
    after = lax.broadcasted_iota(jnp.int32, (lanes, lanes), 1)
    same = (before < half) == (after < half)
    return jnp.where(jnp.logical_and(before <= after, same), 1.0, 0.0).astype(BF16)


def earlier_kernel(out):
    out[...] = earlier_tokens(out.shape[0])


def slot_order(ids, gates, masks, cap, upto=None):
    lanes = ids.shape[1]
    half = lanes // 2
    row = lax.broadcasted_iota(jnp.int32, (8, lanes), 0)
    wanted = jnp.full((8, lanes), masks[0], jnp.int32)
    for n in range(1, len(masks)):
        wanted = jnp.where(row == n, masks[n], wanted)
    wanted = jnp.bitwise_xor(lax.axis_index("expert"), wanted)
    hit_0 = ids[0:1] == wanted
    hit_1 = ids[1:2] == wanted
    named = jnp.where(jnp.logical_or(hit_0, hit_1), 1.0, 0.0)
    gate = jnp.where(hit_0, gates[0:1], jnp.where(hit_1, gates[1:2], 0.0))
    if upto is None:
        upto = earlier_tokens(lanes)
    counts = jnp.dot(named.astype(BF16), upto, preferred_element_type=F32)
    slots = jnp.where(named > 0.5, counts.astype(jnp.int32) - 1, -1)
    slot_no = lax.broadcasted_iota(jnp.int32, (cap, lanes), 0)
    in_first = lax.broadcasted_iota(jnp.int32, (cap, lanes), 1) < half
    rows = []
    for n in range(len(masks)):
        match = jnp.where(slots[n : n + 1] == slot_no, 1.0, 0.0)
        rows.append(jnp.where(in_first, match, 0.0))
        rows.append(jnp.where(in_first, 0.0, match))
    return rows, jnp.where(hit_0, 1.0, 0.0), jnp.where(hit_1, 1.0, 0.0), gate


def gate_columns(rows, gate):
    found = [
        jnp.sum(row * gate[n // 2 : n // 2 + 1], axis=1, keepdims=True)
        for n, row in enumerate(rows)
    ]
    found = jnp.concatenate(found, axis=0)
    return jnp.broadcast_to(found, (found.shape[0], GATE_LANES)).astype(BF16)


def near_kernel(
    upto, own_ids, own_gate, own_up, own_act, pair_ids, pair_gate, pair_up, pair_act,
    up_0, near, saved_0, saved_2, saved_3, gate_0, acts,
):
    tokens = own_up.shape[0]
    cap, width = up_0.shape[0] // 2, up_0.shape[1]
    units = own_act.shape[3]
    wide = 2 * units
    ids = jnp.concatenate([own_ids[...], pair_ids[...]], axis=1)
    gates = jnp.concatenate([own_gate[...].astype(F32), pair_gate[...].astype(F32)], axis=1)
    picks = ids.shape[0]
    named = jnp.concatenate([ids.astype(F32), gates], axis=0)
    rest = jnp.zeros((2 * cap - 2 * picks, ids.shape[1]), F32)
    named = jnp.concatenate([named, rest], axis=0)
    saved_2[:, wide:] = named.astype(BF16)
    rows, hit_0, hit_1, gate = slot_order(ids, gates, (0, 2, 4, 6), cap, upto[...])
    order_bf = jnp.concatenate(rows, axis=0).astype(BF16)
    gates = gate_columns(rows[:4], gate)
    gate_0[...] = gates[: 2 * cap]
    near[:, width : width + GATE_LANES] = gates[2 * cap :]
    sel_0 = jnp.concatenate([rows[n] * hit_0[n // 2 : n // 2 + 1] for n in range(8)], axis=0)
    sel_1 = jnp.concatenate([rows[n] * hit_1[n // 2 : n // 2 + 1] for n in range(8)], axis=0)
    sel = jnp.concatenate([sel_0.astype(BF16), sel_1.astype(BF16)], axis=1)
    ups = jnp.concatenate([own_up[...], pair_up[...]], axis=0)
    picked = jnp.dot(order_bf[: 4 * cap], ups, preferred_element_type=F32)
    up_0[...] = picked[: 2 * cap].astype(BF16)
    near[:, :width] = picked[2 * cap :].astype(BF16)
    for block, act in enumerate((own_act, pair_act)):
        for pick in range(picks):
            low = (2 * pick + block) * tokens
            for side in range(2):
                part = act[:, pick, side, :]
                acts[low : low + tokens, side * units : (side + 1) * units] = part
    got = jnp.dot(sel, acts[...], preferred_element_type=F32)
    low = near.shape[1] - wide
    for n, (out, lane) in enumerate(((saved_0, 0), (near, low), (saved_2, 0), (saved_3, 0))):
        out[:, lane : lane + wide] = got[2 * cap * n : 2 * cap * (n + 1)].astype(BF16)


def read_routes(routes):
    named = routes.astype(F32)
    return named[:2].astype(jnp.int32), named[2:4]


def far_kernel(saved_2, both_up, up_2, up_3, gate_2):
    cap, width = up_2.shape[0] // 2, up_2.shape[1]
    tokens = both_up.shape[0] // 2
    ids, gates = read_routes(saved_2[:, saved_2.shape[1] - 2 * tokens :])
    rows, _, _, gate = slot_order(ids, gates, (0, 2), cap)
    order = jnp.concatenate(rows, axis=0)
    odd = lax.axis_index("expert") % 2 == 1
    order = jnp.where(odd, pltpu.roll(order, tokens, 1), order).astype(BF16)
    picked = jnp.dot(order, both_up[...], preferred_element_type=F32)
    gates = gate_columns(rows, gate)
    up_2[...] = picked[: 2 * cap].astype(BF16)
    up_3[:, :width] = picked[2 * cap :].astype(BF16)
    up_3[:, width:] = gates[2 * cap :]
    gate_2[...] = gates[: 2 * cap]


def through_expert(up, saved, gate, w_down, w_gate, w_up):
    units = w_down.shape[0]
    gate = gate[:, :1].astype(F32)
    by_a, by_b, both = factors(saved[:, :units], saved[:, units:])
    grad_h = lax.dot_general(up, w_down[...], LAST, preferred_element_type=F32) * gate
    grad_a = (grad_h * by_a).astype(BF16)
    grad_b = (grad_h * by_b).astype(BF16)
    back = lax.dot_general(grad_a, w_gate[...], LAST, preferred_element_type=F32)
    back = back + lax.dot_general(grad_b, w_up[...], LAST, preferred_element_type=F32)
    return back.astype(BF16), (gate * both).astype(BF16)


def own_kernel(up, saved, gate, beside, w_down, w_gate, w_up, back_out, scaled_out):
    width, wide = up.shape[1], saved.shape[1]
    back, scaled = through_expert(up[...], saved[...], gate[...], w_down, w_gate, w_up)
    back_out[:, :width] = back
    back_out[:, width:] = beside[:, wide:]
    scaled_out[...] = scaled


def two_kernel(up, saved, gate, w_down, w_gate, w_up, back_out, scaled_out):
    wide = 2 * w_down.shape[0]
    back, scaled = through_expert(up[...], saved[:, :wide], gate[...], w_down, w_gate, w_up)
    back_out[...] = back
    scaled_out[...] = scaled


def factors(gate_pre, up_pre):
    gate_pre, up_pre = gate_pre.astype(F32), up_pre.astype(F32)
    sig = 1.0 / (1.0 + jnp.exp(-gate_pre))
    silu = gate_pre * sig
    return up_pre * sig * (1.0 + gate_pre * (1.0 - sig)), silu, silu * up_pre


def factors_kernel(near, saved, by_a, by_b, both):
    units = by_a.shape[1]
    low = near.shape[1] - 2 * units
    gate_pre = jnp.concatenate([near[:, low : low + units], saved[:, :units]], axis=0)
    up_pre = jnp.concatenate([near[:, low + units :], saved[:, units:]], axis=0)
    by_a[...], by_b[...], both[...] = factors(gate_pre, up_pre)


def odd_kernel(
    near, up_3, by_a, by_b, both, w_down, w_gate, w_up, back_1, back_6, back_7, scaled_out
):
    each, width = back_1.shape
    gate = [near[:, width : width + 1].astype(F32), up_3[:, width : width + 1].astype(F32)]
    gate = jnp.concatenate(gate, axis=0)
    up = jnp.concatenate([near[:, :width], up_3[:, :width]], axis=0)
    grad_h = lax.dot_general(up, w_down[...], LAST, preferred_element_type=F32) * gate
    grad_a = (grad_h * by_a[...]).astype(BF16)
    grad_b = (grad_h * by_b[...]).astype(BF16)
    scaled_out[...] = (gate * both[...]).astype(BF16)
    back = lax.dot_general(grad_a, w_gate[...], LAST, preferred_element_type=F32)
    back = back + lax.dot_general(grad_b, w_up[...], LAST, preferred_element_type=F32)
    back_1[...] = back[:each].astype(BF16)
    half = each // 2
    back_6[...] = back[each : each + half].astype(BF16)
    back_7[...] = back[each + half :].astype(BF16)


def down_kernel(scaled_a, scaled_b, scaled_c, up_a, up_b, up_c, up_d, out):
    scaled = jnp.concatenate([scaled_a[...], scaled_b[...], scaled_c[...]], axis=0)
    ups = jnp.concatenate([up_a[...], up_b[...], up_c[...], up_d[...]], axis=0)
    out[...] = lax.dot_general(scaled, ups, FIRST, preferred_element_type=F32).astype(BF16)


def two_sum_kernel(rows_0, rows_2, part, order_1, order_67):
    width = part.shape[1]
    ids, gates = read_routes(rows_0[:, width:])
    order = slot_order(ids, gates, (0, 4, 2, 6, 7), rows_2.shape[0] // 2)[0]
    order_1[...] = jnp.concatenate(order[4:6], axis=0).astype(BF16)
    order_67[...] = jnp.concatenate([order[6], order[8]], axis=0).astype(BF16)
    order = jnp.concatenate(order[:4], axis=0).astype(BF16)
    rows = jnp.concatenate([rows_0[:, :width], rows_2[...]], axis=0)
    part[...] = lax.dot_general(order, rows, FIRST, preferred_element_type=F32)


def sum_kernel(order, part, rows_1, own, other):
    tokens = own.shape[0]
    back = lax.dot_general(order[...], rows_1[...], FIRST, preferred_element_type=F32)
    back = part[...] + back
    own[...] = back[:tokens]
    other[...] = back[tokens:].astype(BF16)


def three_sum_kernel(order, rows_6, rows_7, part):
    tokens = part.shape[0]
    rows = jnp.concatenate([rows_6[...].astype(F32), rows_7[...].astype(F32)], axis=0)
    back = lax.dot_general(order[...], rows.astype(BF16), FIRST, preferred_element_type=F32)
    part[...] = back[:tokens]


def last_kernel(own, other, part, out):
    out[...] = (own[...] + other[...].astype(F32) + part[...]).astype(BF16)


def local_call(kernel, outs, args, scratch=(), cost=0, limit=28, **blocks):
    whole = pl.BlockSpec(memory_space=pltpu.VMEM)
    if not blocks:
        blocks["in_specs"] = [whole] * len(args)
        blocks["out_specs"] = [whole] * len(outs)
    return pl.pallas_call(
        kernel,
        out_shape=outs,
        scratch_shapes=scratch,
        compiler_params=pltpu.CompilerParams(vmem_limit_bytes=limit * 1024 * 1024),
        cost_estimate=pl.CostEstimate(flops=cost, bytes_accessed=0, transcendentals=0),
        **blocks,
    )(*args)


def after(value, *others):
    return lax.optimization_barrier((value,) + others)[0]


def before_section(value, mask):
    sections, count = lax.axis_size("section"), lax.axis_size("expert")
    pairs = [
        (s * count + e, (s + sections - 1) % sections * count + (e ^ mask))
        for s in range(sections)
        for e in range(count)
    ]
    return lax.ppermute(value, ("section", "expert"), pairs)


def on_device_pairs(grad_out, pre_act, route_ids, route_gate, w_gate, w_up, w_down):
    tokens, width = grad_out.shape[1:]
    units = w_down.shape[1]
    wide = 2 * units
    cap = 3 * tokens // 8
    upstream = grad_out[0]

    def shape(rows, lanes):
        return jax.ShapeDtypeStruct((rows, lanes), BF16)

    up, act = grad_out[0], pre_act[0]
    ids, gate = route_ids[0].T, route_gate[0].T
    far_up = swapped(up, 4)
    (upto,) = local_call(earlier_kernel, [shape(2 * tokens, 2 * tokens)], (), cost=K0_COST)
    own_rows, near_rows, saved_0, saved_2, saved_3, gate_0 = local_call(
        near_kernel,
        [shape(2 * cap, width), shape(2 * cap, width + GATE_LANES + wide)]
        + [shape(2 * cap, wide), shape(2 * cap, wide + 2 * tokens), shape(2 * cap, wide)]
        + [shape(2 * cap, GATE_LANES)],
        (upto, ids, gate, up, act, swapped(ids, 1), swapped(gate, 1), swapped(up, 1), swapped(act, 1)),
        [pltpu.VMEM((4 * tokens, wide), BF16)],
    )
    near_rows = swapped(near_rows, 2)
    beside, saved_2 = saved_2, swapped(saved_2, 4)
    weights = (w_down[0], w_gate[0], w_up[0])
    back_0, scaled_0 = local_call(
        own_kernel,
        [shape(2 * cap, width + 2 * tokens), shape(2 * cap, units)],
        (own_rows, saved_0, gate_0, beside, *weights),
    )
    far_up = after(far_up, back_0)
    far_both = lax.all_gather(
        far_up, "expert", axis=0, tiled=True, axis_index_groups=[[i, i + 1] for i in range(0, 8, 2)]
    )
    saved_3 = swapped(after(saved_3, far_both), 6)
    two_rows, three_rows, gate_2 = local_call(
        far_kernel,
        [shape(2 * cap, width), shape(2 * cap, width + GATE_LANES), shape(2 * cap, GATE_LANES)],
        (saved_2, far_both),
    )
    three_rows = swapped(three_rows, 2)
    home_0 = before_section(back_0, 0)
    two_rows = after(two_rows, home_0)
    back_2, scaled_2 = local_call(
        two_kernel,
        [shape(2 * cap, width), shape(2 * cap, units)],
        (two_rows, saved_2, gate_2, *weights),
    )
    saved_3 = after(saved_3, back_2)
    by_saved = local_call(
        factors_kernel,
        [jax.ShapeDtypeStruct((4 * cap, units), F32)] * 3,
        (near_rows, saved_3),
        cost=FACTORS_COST,
    )
    back_1, back_6, back_7, scaled_13 = local_call(
        odd_kernel,
        [shape(2 * cap, width)] + [shape(cap, width)] * 2 + [shape(4 * cap, units)],
        (near_rows, three_rows, *by_saved, *weights),
    )
    home_2 = before_section(back_2, 4)
    home_1 = before_section(back_1, 2)
    rows_6 = before_section(back_6, 6)
    rows_7 = before_section(back_7, 7)
    parts = 4

    def columns(array):
        return pl.BlockSpec((array.shape[0], width // parts), lambda n: (0, n))

    def every(array):
        return pl.BlockSpec(array.shape, lambda n: (0, 0))

    scaled = (scaled_0, scaled_2, scaled_13)
    ups = (own_rows, two_rows, near_rows, three_rows)
    (down,) = local_call(
        down_kernel,
        [shape(units, width)],
        scaled + ups,
        grid=(parts,),
        in_specs=[every(a) for a in scaled] + [columns(a) for a in ups],
        out_specs=[pl.BlockSpec((units, width // parts), lambda n: (0, n))],
    )
    home_2 = after(home_2, down)
    part, order_1, order_67 = local_call(
        two_sum_kernel,
        [jax.ShapeDtypeStruct((2 * tokens, width), F32)]
        + [shape(2 * cap, 2 * tokens)] * 2,
        (home_0, home_2),
    )
    rows_6 = after(rows_6, part)
    summed, other = local_call(
        sum_kernel,
        [jax.ShapeDtypeStruct((tokens, width), F32), shape(tokens, width)],
        (order_1, part, home_1),
    )
    other = swapped(other, 1)
    (three,) = local_call(
        three_sum_kernel,
        [jax.ShapeDtypeStruct((tokens, width), F32)],
        (order_67, rows_6, rows_7),
        cost=THREE_COST,
    )
    (total,) = local_call(last_kernel, [shape(tokens, width)], (summed, other, three))
    return total[None], down[None]


def on_device(*args):
    if lax.axis_size("expert") == EXPERTS:
        return on_device_pairs(*args)
    return on_device_general(*args)


def solution(mesh):
    placed = (
        P("section", "expert", None),
        P("section", "expert", None, None, None),
        P("section", "expert", None),
        P("section", "expert", None),
        P("section", None, "expert"),
        P("section", None, "expert"),
        P("section", "expert", None),
    )
    return jax.shard_map(
        on_device,
        mesh=mesh,
        in_specs=placed,
        out_specs=(P("section", "expert", None), P("section", "expert", None)),
        check_vma=False,
    )
```
